256 devices in a mesh: section: 8 (over x, core), ep: 32 (over z, y).
Axes of the slice: x: 4, y: 4, z: 8, core: 2. Of those that a mesh axis runs over, the one named last changes fastest.
Arguments:
- spans: bfloat16 [8, 256, 3584], P(None, 'ep'), may hold values from -6 to 6
- attn_gain: float32 [8, 3584], P('section'), may hold values from 0.25 to 1.75
- kv_gain: float32 [8, 512], P('section'), may hold values from 0.25 to 1.75
- moe_gain: float32 [8, 3584], P('section'), may hold values from 0.25 to 1.75
- w_latent: bfloat16 [8, 3584, 576], P('section', 'ep'), may hold values from -0.09375 to 0.09375
- w_gate: bfloat16 [8, 3584, 16384], P('section', None, 'ep'), may hold values from -0.09375 to 0.09375
- w_up: bfloat16 [8, 3584, 16384], P('section', None, 'ep'), may hold values from -0.09375 to 0.09375
- w_down: bfloat16 [8, 16384, 3584], P('section', 'ep'), may hold values from -0.125 to 0.125
- expert_ids: int32 [8, 8, 256, 2], P('section'), may hold values from 0 to 7, all different within a row; in each aligned block of 8 rows (0 to 7, 8 to 15, ..., all dimensions but the last counted through in order) at most 4 rows name the same one
- gate_vals: float32 [8, 8, 256, 2], P('section', None, 'ep'), may hold values from 0.2 to 1
- owner_map: int32 [8, 8, 64], P('section'), may hold values from 0 to 63, each once within a row
- offsets: int32 [8], replicated, may hold values from 0 to 130816
Outputs:
- states: bfloat16 [8, 256, 3584], P('section', 'ep')
- kv_cache: bfloat16 [8, 8, 256, 576], P('section', None, 'ep')
The draws below stay inside these ranges and needn't reach their ends.
Inputs may be any that keep to these rules, and one draw needn't show every extreme that they name: `expert_ids`: each token's 2 ids are different. In each aligned block of 8 tokens of one span and layer (the rows of one device), no expert is picked by more than 4 tokens, a bound that some block reaches. `owner_map`: each row of 64 entries is a permutation.
All inputs are finite; a program needn't handle non-finite values.
Results may differ from the reference program's by a relative error of at most 0.029.
Values may be sent and summed in bfloat16 or wider, within the bound.
No kernel may reach another device: no remote copies, remote signals or barrier semaphores. Data moves between devices by JAX's collectives and lax.ppermute only.
A program may use at most 64 MiB of HBM per device.

```python
import math
import jax
import jax.numpy as jnp
import numpy as np
from jax import lax

D = 3584
HID = 2048
LAT = 512
EXP_SPLIT = 4
TOPK = 2
KVBLK = 4
SPAN_DEV = 8
EXPERTS = 8
NCHUNK = 8
SPAN_TOK = 256
CAP = 4
HID_DEV = 512
KV = 576
NBLK = 64
N_SECTION = 8
N_EP = 32


def touch_ends(result, key, low, high):
    longest = result.shape.index(max(result.shape))
    spots = []
    for shift in (0, 1):
        where = [jax.random.randint(jax.random.fold_in(key, axis), (), 0, length) for axis, length in enumerate(result.shape)]
        where[longest] = (where[longest] + shift) % result.shape[longest]
        spots.append(tuple(where))
    return result.at[spots[0]].set(low).at[spots[1]].set(high)


def shard_levels(rng, extent, pieces, smallest, largest):
    gain, own = 1.0, jax.random.fold_in(rng, 6)
    for position, parts in pieces:
        steps = jnp.exp(jax.random.uniform(jax.random.fold_in(own, position), (parts,), jnp.float32, smallest / len(pieces), largest / len(pieces)))
        gain = gain * jnp.repeat(steps, extent[position] // parts).reshape([-1 if axis == position else 1 for axis in range(len(extent))])
    return gain


def shared_out(stream_key, own, number, rows, count, top, reach, slope):
    ranking = jax.random.permutation(stream_key, count)
    heavy_load, common = shares(count, rows * top, reach, slope, True), shares(count, rows * top, reach, slope, False)
    places = jnp.arange(count)

    def named(lengths, offset_by):
        used = int((lengths > 0).sum())
        fixed = max(1, used // 4)
        moved = fixed + (places - fixed + offset_by * (used - fixed)) % max(1, count - fixed)
        return jnp.zeros((count,), jnp.int32).at[ranking[jnp.where(places < fixed, places, moved)]].set(jnp.asarray(lengths, jnp.int32))

    lengths = jnp.where(number % 4 == 0, named(heavy_load, number // 4), named(common, number - number // 4 - 1))
    mixed = jax.random.permutation(jax.random.fold_in(own, 3), count)
    source_of, taker = mixed[0:count // 2 * 2:2], mixed[1:count // 2 * 2:2]
    room = jnp.minimum(lengths[source_of] - 1, reach - lengths[taker]) // 2
    room = jnp.where((source_of == ranking[0]) | (taker == ranking[0]) | (lengths[taker] == 0), 0, jnp.maximum(room, 0))
    moved = jax.random.randint(jax.random.fold_in(own, 4), (count // 2,), 0, 1 << 20) % (room + 1)
    lengths = lengths.at[source_of].add(-moved).at[taker].add(moved)
    members = jnp.searchsorted(jnp.cumsum(lengths), jnp.arange(rows * top), side="right").astype(jnp.int32)
    table = members.reshape(top, rows).T
    table = table[jax.random.permutation(jax.random.fold_in(own, 1), rows)]
    offset_by = jax.random.randint(jax.random.fold_in(own, 2), (rows, 1), 0, top)
    return jnp.take_along_axis(table, (jnp.arange(top)[None, :] + offset_by) % top, axis=1)


def shares(number_of, total, bound, skew, full):
    weights = [(1 << 20) // math.isqrt(standing ** skew) + 1 for standing in range(1, number_of + 1)]
    largest = bound if full else min(bound, max(-(-total // number_of), total * weights[0] // sum(weights)))
    least = 1 if total - largest >= number_of - 1 else 0
    holding, spare = [largest] + [least] * (number_of - 1), total - largest - least * (number_of - 1)
    while spare > 0:
        free = [i for i in range(1, number_of) if holding[i] < largest] or [i for i in range(1, number_of) if holding[i] < bound]
        mass, left = sum([weights[i] for i in free]), spare
        for i in free:
            more = min(bound - holding[i], max(1, left * weights[i] // mass), spare)
            holding[i] = holding[i] + more
            spare = spare - more
    return np.array(holding)


def scatter_about(key, extent, deviation, bound, split=(), held_as=jnp.bfloat16):
    factor_of = shard_levels(key, extent, split, -0.22, 0.18) if split else 1.0
    result = jax.random.normal(key, extent, jnp.float32) * deviation * factor_of
    return jnp.minimum(jnp.maximum(result, -bound), bound).astype(held_as)


def setup_inputs(seed: int = 0) -> dict:
    arg_keys = jax.random.split(jax.random.key(seed), 13)
    spans = scatter_about(arg_keys[0], (NCHUNK, SPAN_TOK, D), 1.0, 6.0, ((1, 32),))
    attn_gain = jnp.clip(1.0 + 0.15 * jax.random.normal(arg_keys[1], (N_SECTION, D), jnp.float32), 0.25, 1.75)
    kv_gain = jnp.clip(1.0 + 0.15 * jax.random.normal(arg_keys[2], (N_SECTION, LAT), jnp.float32), 0.25, 1.75)
    moe_gain = jnp.clip(1.0 + 0.15 * jax.random.normal(arg_keys[3], (N_SECTION, D), jnp.float32), 0.25, 1.75)
    w_latent = scatter_about(arg_keys[4], (N_SECTION, D, KV), D ** -0.5, 0.09375, ((0, 8), (1, 32)))
    w_gate = scatter_about(arg_keys[5], (N_SECTION, D, EXPERTS * HID), D ** -0.5, 0.09375, ((0, 8), (2, 32)))
    w_up = scatter_about(arg_keys[6], (N_SECTION, D, EXPERTS * HID), D ** -0.5, 0.09375, ((0, 8), (2, 32)))
    w_down = scatter_about(arg_keys[7], (N_SECTION, EXPERTS * HID, D), HID ** -0.5, 0.125, ((0, 8), (1, 32)))
    expert_ids_keys = jax.random.split(jax.random.fold_in(arg_keys[8], 1), N_SECTION * NCHUNK * SPAN_TOK // SPAN_DEV)
    expert_ids_turns = jax.random.permutation(jax.random.fold_in(arg_keys[8], 3), N_SECTION * NCHUNK * SPAN_TOK // SPAN_DEV)
    expert_ids = jax.vmap(lambda own, number: shared_out(jax.random.fold_in(arg_keys[8], 2), own, number, SPAN_DEV, EXPERTS, TOPK, CAP, 2))(expert_ids_keys, expert_ids_turns).reshape((N_SECTION, NCHUNK, SPAN_TOK, TOPK))
    gate_vals = jnp.clip(0.2 + 0.8 * jax.random.uniform(arg_keys[9], (N_SECTION, NCHUNK, SPAN_TOK, TOPK), jnp.float32) ** shard_levels(arg_keys[9], (N_SECTION, NCHUNK, SPAN_TOK, TOPK), ((0, 8), (2, 32)), -0.2, 0.2), 0.2, 1.0)
    owner_map = jax.vmap(lambda own: jax.random.permutation(own, NBLK))(jax.random.split(arg_keys[10], N_SECTION * NCHUNK)).reshape((N_SECTION, NCHUNK, NBLK)).astype(jnp.int32)
    offsets = touch_ends(jax.random.randint(arg_keys[11], (NCHUNK,), 0, 131072 - SPAN_TOK + 1), jax.random.fold_in(arg_keys[11], 1), 0, 131072 - SPAN_TOK).astype(jnp.int32)
    return dict(spans=spans, attn_gain=attn_gain, kv_gain=kv_gain, moe_gain=moe_gain, w_latent=w_latent, w_gate=w_gate, w_up=w_up, w_down=w_down, expert_ids=expert_ids, gate_vals=gate_vals, owner_map=owner_map, offsets=offsets)


eps = 1e-06

def rms_scale(values, gain_vec):
    values = values.astype(jnp.float32)
    return values * lax.rsqrt(lax.optimization_barrier(jnp.mean(values * values, axis=-1, keepdims=True)) + eps) * gain_vec

def rotate_pairs(rope_part, positions):
    half_dim = rope_part.shape[-1] // 2
    frequency = 10000.0 ** (-jnp.arange(half_dim, dtype=jnp.float32) / half_dim)
    angles = positions.astype(jnp.float32)[:, None] * frequency[None, :]
    cosine = jnp.cos(angles)
    sine_part = jnp.sin(angles)
    first_half = rope_part[:, :half_dim]
    second = rope_part[:, half_dim:]
    return jnp.concatenate([first_half * cosine - second * sine_part, second * cosine + first_half * sine_part], axis=1)

def latent_rows(latent, gain_vec, positions):
    compressed = rms_scale(latent[:, :LAT], gain_vec)
    rotated = rotate_pairs(latent[:, LAT:], positions)
    return jnp.concatenate([compressed, rotated], axis=1).astype(jnp.bfloat16)

def expert_block(normed, route_ids, gates, expert, layer_gate, layer_up, layer_down):
    matches = route_ids == expert
    picked = jnp.any(matches, axis=1)
    weights = lax.optimization_barrier(jnp.sum(jnp.where(matches, gates, 0.0), axis=1))
    slot_index = jnp.nonzero(picked, size=N_EP * CAP, fill_value=0)[0]
    is_valid = (jnp.arange(N_EP * CAP) < jnp.sum(picked.astype(jnp.int32))).astype(jnp.float32)
    token_rows = normed[slot_index]
    col_start = expert * HID
    gate_proj = jnp.dot(token_rows, lax.dynamic_slice_in_dim(layer_gate, col_start, HID, 1), preferred_element_type=jnp.float32)
    up_proj = jnp.dot(token_rows, lax.dynamic_slice_in_dim(layer_up, col_start, HID, 1), preferred_element_type=jnp.float32)
    hidden = (jax.nn.silu(gate_proj) * up_proj).astype(jnp.bfloat16)
    expert_sum = jnp.zeros((token_rows.shape[0], D), jnp.float32)
    for part_id in range(EXP_SPLIT):
        part_start = part_id * HID_DEV
        down_rows = lax.dynamic_slice_in_dim(layer_down, col_start + part_start, HID_DEV, 0)
        down_part = jnp.dot(hidden[:, part_start:part_start + HID_DEV], down_rows, preferred_element_type=jnp.float32).astype(jnp.bfloat16)
        expert_sum = expert_sum + down_part.astype(jnp.float32)
    row_scale = weights[slot_index] * is_valid
    return (slot_index, row_scale[:, None] * expert_sum)

def reference(spans, attn_gain, kv_gain, moe_gain, w_latent, w_gate, w_up, w_down, expert_ids, gate_vals, owner_map, offsets):
    blank_rows = jnp.zeros((SPAN_TOK, KV), jnp.bfloat16)
    kv_table = [[blank_rows for span_id in range(NCHUNK)] for layer_id in range(N_SECTION)]
    finals = [blank_rows for layer_id in range(N_SECTION)]
    for span_id in range(NCHUNK):
        tokens = spans[span_id]
        positions = offsets[span_id] + jnp.arange(SPAN_TOK, dtype=jnp.int32)
        for layer_id in range(NCHUNK - span_id):
            normed_kv = rms_scale(tokens, attn_gain[layer_id]).astype(jnp.bfloat16)
            latent = jnp.dot(normed_kv, w_latent[layer_id], preferred_element_type=jnp.float32)
            kv_rows = latent_rows(latent, kv_gain[layer_id], positions)
            blocks = kv_rows.reshape(NBLK, KVBLK, KV)
            kv_table[layer_id][span_id] = jnp.take(blocks, owner_map[layer_id, span_id], axis=0).reshape(SPAN_TOK, KV)
            normed_moe = rms_scale(tokens, moe_gain[layer_id]).astype(jnp.bfloat16)
            route_ids = expert_ids[layer_id, span_id]
            gates = gate_vals[layer_id, span_id]
            layer_gate = w_gate[layer_id]
            layer_up = w_up[layer_id]
            layer_down = w_down[layer_id]

            def add_expert(expert, moe_sum, normed_moe=normed_moe, route_ids=route_ids, gates=gates, layer_gate=layer_gate, layer_up=layer_up, layer_down=layer_down):
                slot_index, contrib = expert_block(normed_moe, route_ids, gates, expert, layer_gate, layer_up, layer_down)
                return moe_sum.at[slot_index].add(contrib)
            moe_sum = lax.fori_loop(0, EXPERTS, add_expert, jnp.zeros((SPAN_TOK, D), jnp.float32))
            tokens = (tokens.astype(jnp.float32) + moe_sum).astype(jnp.bfloat16)
        finals[NCHUNK - 1 - span_id] = tokens
    return (jnp.stack(finals), jnp.stack([jnp.stack(table_row) for table_row in kv_table]))
```

```python
import jax
import jax.numpy as jnp
from jax import lax
from jax.sharding import Mesh, PartitionSpec as P

LAT = 512
EXP_SPLIT = 4
TOPK = 2
KVBLK = 4
EARLY = 6


eps = 1e-06


def shifted(block, axis, distance):
    devices = range(lax.axis_size(axis))
    route = [(i - distance, i) for i in devices if i - distance in devices]
    return lax.ppermute(block, axis, route)


def rms_scale(values, gain_vec):
    values = values.astype(jnp.float32)
    return values * lax.rsqrt(jnp.mean(values * values, axis=-1, keepdims=True) + eps) * gain_vec


def rotate_pairs(rope_part, positions):
    half_dim = rope_part.shape[-1] // 2
    frequency = 10000.0 ** (-jnp.arange(half_dim, dtype=jnp.float32) / half_dim)
    angles = positions.astype(jnp.float32)[:, None] * frequency[None, :]
    cosine = jnp.cos(angles)
    sine_part = jnp.sin(angles)
    first_half = rope_part[:, :half_dim]
    second = rope_part[:, half_dim:]
    return jnp.concatenate(
        [first_half * cosine - second * sine_part, second * cosine + first_half * sine_part], axis=1
    )


def latent_rows(latent, gain_vec, positions):
    compressed = rms_scale(latent[:, :LAT], gain_vec)
    rotated = rotate_pairs(latent[:, LAT:], positions)
    return jnp.concatenate([compressed, rotated], axis=1).astype(jnp.bfloat16)


def packing(route_ids, expert_list, capacity):
    matches = route_ids[:, :, None, :] == expert_list[None, None, :, None]
    picked = jnp.any(matches, axis=3).astype(jnp.int32)
    slot_rank = jnp.cumsum(picked, axis=1) - 1
    slot_ids = jnp.arange(capacity, dtype=jnp.int32)
    slot_table = (slot_rank[..., None] == slot_ids) & (picked[..., None] > 0)
    return jnp.transpose(slot_table, (0, 2, 3, 1))


def expert_slice(token_rows, local_gate, local_up, local_down):
    gate_proj = jnp.dot(token_rows, local_gate, preferred_element_type=jnp.float32)
    up_proj = jnp.dot(token_rows, local_up, preferred_element_type=jnp.float32)
    hidden = (jax.nn.silu(gate_proj) * up_proj).astype(jnp.bfloat16)
    return jnp.dot(hidden, local_down, preferred_element_type=jnp.float32).astype(jnp.bfloat16)


def body(
    spans,
    attn_gain,
    kv_gain,
    moe_gain,
    w_latent,
    w_gate,
    w_up,
    w_down,
    expert_ids,
    gate_vals,
    owner_map,
    offsets,
):
    section_id = lax.axis_index("section")
    plane = lax.axis_index("z")
    column = lax.axis_index("y")
    n_planes = lax.axis_size("z")
    n_columns = lax.axis_size("y")
    member = plane * n_columns + column
    n_members = n_planes * n_columns
    n_sections = lax.axis_size("section")
    n_spans, span_dev, model_width = spans.shape
    kv_width = w_latent.shape[2]
    experts = n_members // EXP_SPLIT
    capacity = min(span_dev, 2 * span_dev * TOPK // experts)
    per_owner = span_dev // KVBLK
    all_experts = jnp.arange(experts, dtype=jnp.int32)
    local_gate = w_gate[0]
    local_up = w_up[0]
    local_down = w_down[0]
    latent_full = lax.all_gather(w_latent[0], ("z", "y"), axis=0, tiled=True)

    ticks = jnp.arange(n_sections, dtype=jnp.int32)
    tick_span = jnp.clip(ticks - section_id, 0, n_spans - 1)
    own_ids = lax.dynamic_slice_in_dim(expert_ids[0], member * span_dev, span_dev, 1)
    own_ids = jnp.take(own_ids, tick_span, axis=0)
    gate_rows = jnp.take(gate_vals[0], tick_span, axis=0)
    own_table = packing(own_ids, all_experts, capacity)
    gate_for = jnp.sum(
        jnp.where(
            own_ids[..., None] == all_experts[None, None, None, :], gate_rows[..., None], 0.0
        ),
        axis=2,
    )
    weighting = own_table.astype(jnp.float32) * jnp.transpose(gate_for, (0, 2, 1))[:, :, None, :]
    choose = own_table.astype(jnp.bfloat16).reshape(n_sections, experts * capacity, span_dev)
    weighting = jnp.transpose(
        weighting.reshape(n_sections, experts * capacity, span_dev), (0, 2, 1)
    )
    positions = (
        jnp.take(offsets, tick_span)[:, None]
        + member * span_dev
        + jnp.arange(span_dev, dtype=jnp.int32)[None, :]
    )
    block_order = jnp.take(owner_map[0], tick_span, axis=0)

    def project(first, last):
        rows = jnp.concatenate(tick_rows[first:last], axis=0)
        normed = rms_scale(rows, attn_gain[0]).astype(jnp.bfloat16)
        latent = jnp.dot(normed, latent_full, preferred_element_type=jnp.float32)
        return latent_rows(latent, kv_gain[0], positions[first:last].reshape(-1))

    def deliver_whole(first, last):
        count = last - first
        kv_rows = project(first, last)
        gathered = lax.all_gather(kv_rows, ("z", "y"), axis=0)
        blocks = gathered.reshape(n_members, count, per_owner, KVBLK * kv_width)
        blocks = jnp.transpose(blocks, (1, 0, 2, 3)).reshape(count, -1, KVBLK * kv_width)
        owned = lax.dynamic_slice_in_dim(
            block_order[first:last], member * per_owner, per_owner, 1
        )
        taken = jnp.take_along_axis(blocks, owned[:, :, None], axis=1)
        return taken.reshape(count, span_dev, kv_width)

    def deliver_planes(first, last):
        count = last - first
        kv_rows = project(first, last).reshape(count, per_owner, KVBLK * kv_width)
        column_rows = lax.all_gather(kv_rows, "y", axis=1, tiled=True)
        held = plane * n_columns * per_owner + jnp.arange(n_columns * per_owner, dtype=jnp.int32)
        wanted = block_order[first:last].reshape(count, n_planes, n_columns, per_owner)
        wanted = lax.dynamic_index_in_dim(wanted, column, 2, keepdims=False)
        pick = (wanted[..., None] == held).astype(jnp.bfloat16)
        packed = jnp.einsum(
            "tpib,tbk->ptik", pick, column_rows, preferred_element_type=jnp.float32
        ).astype(jnp.bfloat16)
        arrived = lax.all_to_all(packed, "z", split_axis=0, concat_axis=0, tiled=True)
        taken = jnp.sum(arrived.astype(jnp.float32), axis=0).astype(jnp.bfloat16)
        return taken.reshape(count, span_dev, kv_width)

    tick_rows = []
    delivered = []
    layer_in = jnp.zeros((span_dev, model_width), jnp.bfloat16)
    for tick in range(n_sections):
        tokens = jnp.where(section_id == 0, spans[tick], layer_in)
        tick_rows.append(tokens)
        if tick == EARLY:
            delivered.append(deliver_whole(0, EARLY))
        normed_moe = rms_scale(tokens, moe_gain[0]).astype(jnp.bfloat16)
        chosen = jnp.dot(
            choose[tick], normed_moe, preferred_element_type=jnp.float32
        ).astype(jnp.bfloat16)
        arrived = lax.all_to_all(chosen, "z", split_axis=0, concat_axis=0, tiled=True)
        token_rows = lax.all_gather(arrived, "y", axis=0, tiled=True)
        parts = expert_slice(token_rows, local_gate, local_up, local_down)
        quarters = lax.all_to_all(parts, "y", split_axis=0, concat_axis=0, tiled=True)
        summed = jnp.sum(
            quarters.reshape(n_columns, -1, model_width).astype(jnp.float32), axis=0
        ).astype(jnp.bfloat16)
        returned = lax.all_to_all(summed, "z", split_axis=0, concat_axis=0, tiled=True)
        moe_sum = jnp.dot(
            weighting[tick], returned.astype(jnp.float32), precision=lax.Precision.HIGHEST
        )
        layer_out = (tokens.astype(jnp.float32) + moe_sum).astype(jnp.bfloat16)
        if tick + 1 < n_sections:
            layer_in = shifted(layer_out, "section", 1)
    delivered.append(deliver_planes(EARLY, n_sections))
    blank = jnp.zeros((n_spans, span_dev, kv_width), jnp.bfloat16)
    kv_ticks = jnp.concatenate(delivered + [blank], axis=0)
    kv_store = lax.dynamic_slice_in_dim(kv_ticks, section_id, n_spans, 0)
    return (layer_out[None], kv_store[None])


def solution(mesh):
    n_members = mesh.shape["ep"]
    grid = Mesh(
        mesh.devices.reshape(mesh.shape["section"], n_members // EXP_SPLIT, EXP_SPLIT),
        ("section", "z", "y"),
    )
    ep = ("z", "y")
    in_specs = (
        P(None, ep, None),
        P("section", None),
        P("section", None),
        P("section", None),
        P("section", ep, None),
        P("section", None, ep),
        P("section", None, ep),
        P("section", ep, None),
        P("section", None, None, None),
        P("section", None, ep, None),
        P("section", None, None),
        P(),
    )
    out_specs = (P("section", ep, None), P("section", None, ep, None))
    return jax.shard_map(body, mesh=grid, in_specs=in_specs, out_specs=out_specs, check_vma=False)
```

```python
import jax
import jax.numpy as jnp
from jax import lax
from jax.experimental import pallas as pl
from jax.experimental.pallas import tpu as pltpu
from jax.sharding import Mesh, PartitionSpec as P

LAT = 512
EXP_SPLIT = 4
TOPK = 2
KVBLK = 4
EARLY = 6


eps = 1e-06


def shifted(block, axis, distance):
    devices = range(lax.axis_size(axis))
    route = [(i - distance, i) for i in devices if i - distance in devices]
    return lax.ppermute(block, axis, route)


def turned(block, distance, live):
    size = lax.axis_size("y")
    route = [
        (s * size + i, s * size + (i + distance) % size) for s in range(live) for i in range(size)
    ]
    return lax.ppermute(block, ("section", "y"), route)


def rms_scale(values, gain_vec):
    values = values.astype(jnp.float32)
    return values * lax.rsqrt(jnp.mean(values * values, axis=-1, keepdims=True) + eps) * gain_vec


def rotate_pairs(rope_part, positions):
    half_dim = rope_part.shape[-1] // 2
    frequency = 10000.0 ** (-jnp.arange(half_dim, dtype=jnp.float32) / half_dim)
    angles = positions.astype(jnp.float32)[:, None] * frequency[None, :]
    cosine = jnp.cos(angles)
    sine_part = jnp.sin(angles)
    first_half = rope_part[:, :half_dim]
    second = rope_part[:, half_dim:]
    return jnp.concatenate(
        [first_half * cosine - second * sine_part, second * cosine + first_half * sine_part], axis=1
    )


def latent_rows(latent, gain_vec, positions):
    compressed = rms_scale(latent[:, :LAT], gain_vec)
    rotated = rotate_pairs(latent[:, LAT:], positions)
    return jnp.concatenate([compressed, rotated], axis=1).astype(jnp.bfloat16)


def packing(route_ids, expert_list, capacity):
    matches = route_ids[:, :, None, :] == expert_list[None, None, :, None]
    picked = jnp.any(matches, axis=3).astype(jnp.int32)
    slot_rank = jnp.cumsum(picked, axis=1) - 1
    slot_ids = jnp.arange(capacity, dtype=jnp.int32)
    slot_table = (slot_rank[..., None] == slot_ids) & (picked[..., None] > 0)
    return jnp.transpose(slot_table, (0, 2, 3, 1))


def expert_kernel(
    n_chunks, rows, first, second, third, fourth, gate_hbm, up_hbm, down_hbm,
    first_out, second_out, third_out, fourth_out,
    tokens, gate_buf, up_buf, down_buf, gate_sem, up_sem, down_sem,
):
    depth = gate_buf.shape[0] // n_chunks
    width = down_buf.shape[1] // n_chunks
    gate_copies = []
    up_copies = []
    down_copies = []
    for i in range(n_chunks):
        span = pl.ds(i * depth, depth)
        gate_copies.append(
            pltpu.make_async_copy(gate_hbm.at[span, :], gate_buf.at[span, :], gate_sem.at[i])
        )
        up_copies.append(
            pltpu.make_async_copy(up_hbm.at[span, :], up_buf.at[span, :], up_sem.at[i])
        )
        cols = pl.ds(i * width, width)
        down_copies.append(
            pltpu.make_async_copy(down_hbm.at[:, cols], down_buf.at[:, cols], down_sem.at[i])
        )
    for i in range(n_chunks):
        gate_copies[i].start()
        up_copies[i].start()
    for i in range(n_chunks):
        down_copies[i].start()
    for k, chunk in enumerate((first, second, third, fourth)):
        tokens[pl.ds(k * rows, rows), :] = chunk[...]
    gate_proj = jnp.zeros((4 * rows, gate_buf.shape[1]), jnp.float32)
    up_proj = jnp.zeros((4 * rows, gate_buf.shape[1]), jnp.float32)
    for i in range(n_chunks):
        span = pl.ds(i * depth, depth)
        gate_copies[i].wait()
        gate_proj += jnp.dot(
            tokens[:, span], gate_buf[span, :], preferred_element_type=jnp.float32
        )
        up_copies[i].wait()
        up_proj += jnp.dot(tokens[:, span], up_buf[span, :], preferred_element_type=jnp.float32)
    hidden = (gate_proj / (1.0 + jnp.exp(-gate_proj)) * up_proj).astype(jnp.bfloat16)
    for i in range(n_chunks):
        cols = pl.ds(i * width, width)
        down_copies[i].wait()
        part = jnp.dot(hidden, down_buf[:, cols], preferred_element_type=jnp.float32)
        part = part.astype(jnp.bfloat16)
        for k, out in enumerate((first_out, second_out, third_out, fourth_out)):
            out[:, cols] = part[k * rows : (k + 1) * rows, :]


def expert_slice(chunks, local_gate, local_up, local_down):
    rows, model_width = chunks[0].shape
    hidden_width = local_gate.shape[1]
    n_chunks = 7
    flops = 2 * 4 * rows * model_width * hidden_width * 3
    moved = 3 * 2 * model_width * hidden_width
    return pl.pallas_call(
        lambda *refs: expert_kernel(n_chunks, rows, *refs),
        out_shape=[jax.ShapeDtypeStruct((rows, model_width), jnp.bfloat16)] * 4,
        in_specs=[pl.BlockSpec(memory_space=pltpu.VMEM)] * 4
        + [pl.BlockSpec(memory_space=pl.ANY)] * 3,
        out_specs=[pl.BlockSpec(memory_space=pltpu.VMEM)] * 4,
        scratch_shapes=[
            pltpu.VMEM((4 * rows, model_width), jnp.bfloat16),
            pltpu.VMEM((model_width, hidden_width), jnp.bfloat16),
            pltpu.VMEM((model_width, hidden_width), jnp.bfloat16),
            pltpu.VMEM((hidden_width, model_width), jnp.bfloat16),
            pltpu.SemaphoreType.DMA((n_chunks,)),
            pltpu.SemaphoreType.DMA((n_chunks,)),
            pltpu.SemaphoreType.DMA((n_chunks,)),
        ],
        compiler_params=pltpu.CompilerParams(vmem_limit_bytes=40 * 1024 * 1024),
        cost_estimate=pl.CostEstimate(flops=flops, bytes_accessed=moved, transcendentals=0),
    )(*chunks, local_gate, local_up, local_down)


def body(
    spans,
    attn_gain,
    kv_gain,
    moe_gain,
    w_latent,
    w_gate,
    w_up,
    w_down,
    expert_ids,
    gate_vals,
    owner_map,
    offsets,
):
    section_id = lax.axis_index("section")
    plane = lax.axis_index("z")
    column = lax.axis_index("y")
    n_planes = lax.axis_size("z")
    n_columns = lax.axis_size("y")
    member = plane * n_columns + column
    n_members = n_planes * n_columns
    n_sections = lax.axis_size("section")
    n_spans, span_dev, model_width = spans.shape
    kv_width = w_latent.shape[2]
    experts = n_members // EXP_SPLIT
    capacity = min(span_dev, 2 * span_dev * TOPK // experts)
    per_owner = span_dev // KVBLK
    all_experts = jnp.arange(experts, dtype=jnp.int32)
    local_gate = w_gate[0]
    local_up = w_up[0]
    local_down = w_down[0]
    latent_full = lax.all_gather(w_latent[0], ("z", "y"), axis=0, tiled=True)

    def by_tick(values):
        padded = jnp.concatenate([jnp.zeros_like(values), values], axis=0)
        return lax.dynamic_slice_in_dim(padded, n_spans - section_id, n_sections, 0)

    own_ids = by_tick(lax.dynamic_slice_in_dim(expert_ids[0], member * span_dev, span_dev, 1))
    gate_rows = by_tick(gate_vals[0])
    own_table = packing(own_ids, all_experts, capacity)
    gate_for = jnp.sum(
        jnp.where(
            own_ids[..., None] == all_experts[None, None, None, :], gate_rows[..., None], 0.0
        ),
        axis=2,
    )
    weighting = own_table.astype(jnp.float32) * jnp.transpose(gate_for, (0, 2, 1))[:, :, None, :]
    choose = own_table.astype(jnp.bfloat16).reshape(n_sections, experts * capacity, span_dev)
    weighting = jnp.transpose(
        weighting.reshape(n_sections, experts * capacity, span_dev), (0, 2, 1)
    )
    positions = (
        by_tick(offsets)[:, None]
        + member * span_dev
        + jnp.arange(span_dev, dtype=jnp.int32)[None, :]
    )
    block_order = by_tick(owner_map[0])

    def project(first, last):
        rows = jnp.concatenate(tick_rows[first:last], axis=0)
        normed = rms_scale(rows, attn_gain[0]).astype(jnp.bfloat16)
        latent = jnp.dot(normed, latent_full, preferred_element_type=jnp.float32)
        return latent_rows(latent, kv_gain[0], positions[first:last].reshape(-1))

    def deliver_whole(first, last):
        count = last - first
        kv_rows = project(first, last)
        gathered = lax.all_gather(kv_rows, ("z", "y"), axis=0)
        blocks = gathered.reshape(n_members, count, per_owner, KVBLK * kv_width)
        blocks = jnp.transpose(blocks, (1, 0, 2, 3)).reshape(count, -1, KVBLK * kv_width)
        owned = lax.dynamic_slice_in_dim(
            block_order[first:last], member * per_owner, per_owner, 1
        )
        taken = jnp.take_along_axis(blocks, owned[:, :, None], axis=1)
        return taken.reshape(count, span_dev, kv_width)

    def to_planes(first, last):
        count = last - first
        blocks = project(first, last).reshape(count, per_owner, KVBLK * kv_width)
        held = member * per_owner + jnp.arange(per_owner, dtype=jnp.int32)
        wanted = block_order[first:last].reshape(count, n_planes, 1, n_columns * per_owner)
        pick = (wanted == held[:, None]).any(axis=3).astype(jnp.bfloat16)
        packed = jnp.transpose(pick, (1, 0, 2))[..., None] * blocks[None]
        return lax.all_to_all(packed, "z", split_axis=0, concat_axis=0, tiled=True)

    def to_columns(arrived, first, last, live):
        count = last - first
        held = (
            jnp.arange(n_planes, dtype=jnp.int32)[:, None] * n_columns * per_owner
            + column * per_owner
            + jnp.arange(per_owner, dtype=jnp.int32)[None, :]
        )
        blocks = jnp.transpose(arrived, (1, 0, 2, 3)).reshape(count, -1, KVBLK * kv_width)
        order = block_order[first:last].reshape(count, n_planes, n_columns, per_owner)
        order = lax.dynamic_index_in_dim(order, plane, 1, keepdims=False)
        total = 0.0
        for distance in range(n_columns):
            target = (column + distance) % n_columns
            wanted = lax.dynamic_index_in_dim(order, target, 1, keepdims=False)
            pick = (wanted[..., None] == held.reshape(-1)).astype(jnp.bfloat16)
            packed = jnp.einsum(
                "tib,tbk->tik", pick, blocks, preferred_element_type=jnp.float32
            ).astype(jnp.bfloat16)
            if distance:
                packed = turned(packed, distance, live)
            total = total + packed.astype(jnp.float32)
        return total.astype(jnp.bfloat16).reshape(count, span_dev, kv_width)

    tick_rows = []
    layer_in = jnp.zeros((span_dev, model_width), jnp.bfloat16)
    early = None
    for tick in range(n_sections):
        last_tick = tick + 1 == n_sections
        live = tick + 1
        tokens = jnp.where(section_id == 0, spans[tick], layer_in)
        tick_rows.append(tokens)
        if tick == EARLY:
            early = deliver_whole(0, EARLY)
        normed_moe = rms_scale(tokens, moe_gain[0]).astype(jnp.bfloat16)
        chosen = jnp.dot(
            choose[tick], normed_moe, preferred_element_type=jnp.float32
        ).astype(jnp.bfloat16)
        arrived = lax.all_to_all(chosen, "z", split_axis=0, concat_axis=0, tiled=True)
        chunks = [arrived] + [turned(arrived, k, live) for k in range(1, n_columns)]
        parts = expert_slice(chunks, local_gate, local_up, local_down)
        summed = parts[0].astype(jnp.float32)
        for k in range(1, n_columns):
            summed = summed + turned(parts[k], n_columns - k, live).astype(jnp.float32)
        summed = summed.astype(jnp.bfloat16)
        if last_tick:
            late = to_planes(EARLY, n_sections)
            late = to_columns(late, EARLY, n_sections, live)
        returned = lax.all_to_all(summed, "z", split_axis=0, concat_axis=0, tiled=True)
        moe_sum = jnp.dot(
            weighting[tick], returned.astype(jnp.float32), precision=lax.Precision.HIGHEST
        )
        layer_out = (tokens.astype(jnp.float32) + moe_sum).astype(jnp.bfloat16)
        if not last_tick:
            layer_in = shifted(layer_out, "section", 1)
    delivered = [early, late]
    blank = jnp.zeros((n_spans, span_dev, kv_width), jnp.bfloat16)
    kv_ticks = jnp.concatenate(delivered + [blank], axis=0)
    kv_store = lax.dynamic_slice_in_dim(kv_ticks, section_id, n_spans, 0)
    return (layer_out[None], kv_store[None])


def solution(mesh):
    n_members = mesh.shape["ep"]
    grid = Mesh(
        mesh.devices.reshape(mesh.shape["section"], n_members // EXP_SPLIT, EXP_SPLIT),
        ("section", "z", "y"),
    )
    ep = ("z", "y")
    in_specs = (
        P(None, ep, None),
        P("section", None),
        P("section", None),
        P("section", None),
        P("section", ep, None),
        P("section", None, ep),
        P("section", None, ep),
        P("section", ep, None),
        P("section", None, None, None),
        P("section", None, ep, None),
        P("section", None, None),
        P(),
    )
    out_specs = (P("section", ep, None), P("section", None, ep, None))
    return jax.shard_map(body, mesh=grid, in_specs=in_specs, out_specs=out_specs, check_vma=False)
```

```python
import jax
import jax.numpy as jnp
from jax import lax
from jax.experimental import pallas as pl
from jax.experimental.pallas import tpu as pltpu
from jax.sharding import Mesh, PartitionSpec as P

LAT = 512
EXP_SPLIT = 4
TOPK = 2
KVBLK = 4
EARLY = 7


eps = 1e-06


def shifted(block, axis, distance):
    devices = range(lax.axis_size(axis))
    route = [(i - distance, i) for i in devices if i - distance in devices]
    return lax.ppermute(block, axis, route)


def rms_scale(values, gain_vec):
    values = values.astype(jnp.float32)
    return values * lax.rsqrt(jnp.mean(values * values, axis=-1, keepdims=True) + eps) * gain_vec


def rotate_pairs(rope_part, positions):
    half_dim = rope_part.shape[-1] // 2
    frequency = 10000.0 ** (-jnp.arange(half_dim, dtype=jnp.float32) / half_dim)
    angles = positions.astype(jnp.float32)[:, None] * frequency[None, :]
    cosine = jnp.cos(angles)
    sine_part = jnp.sin(angles)
    first_half = rope_part[:, :half_dim]
    second = rope_part[:, half_dim:]
    return jnp.concatenate(
        [first_half * cosine - second * sine_part, second * cosine + first_half * sine_part], axis=1
    )


def latent_rows(latent, gain_vec, positions):
    compressed = rms_scale(latent[:, :LAT], gain_vec)
    rotated = rotate_pairs(latent[:, LAT:], positions)
    return jnp.concatenate([compressed, rotated], axis=1).astype(jnp.bfloat16)


def packing(route_ids, expert_list, capacity):
    matches = route_ids[:, :, None, :] == expert_list[None, None, :, None]
    picked = jnp.any(matches, axis=3).astype(jnp.int32)
    slot_rank = jnp.cumsum(picked, axis=1) - 1
    slot_ids = jnp.arange(capacity, dtype=jnp.int32)
    slot_table = (slot_rank[..., None] == slot_ids) & (picked[..., None] > 0)
    return jnp.transpose(slot_table, (0, 2, 3, 1))


def one_hot(rows, cols, wanted, kept=None):
    row = lax.broadcasted_iota(jnp.int32, (rows, cols), 0)
    col = lax.broadcasted_iota(jnp.int32, (rows, cols), 1)
    hit = col == wanted(row)
    if kept is not None:
        hit = hit & kept(row)
    return jnp.where(hit, 1.0, 0.0).astype(jnp.bfloat16)


def matmul(left, right):
    return jnp.dot(left, right, preferred_element_type=jnp.float32)


def in_vmem(kernel, out_shape, operands, limit_mib, flops=0, tick=None, tables=()):
    moved = sum(x.size * x.dtype.itemsize for x in operands)
    specs = [pl.BlockSpec(memory_space=pltpu.VMEM)] * len(operands)
    for table in tables:
        specs.append(pl.BlockSpec((1,) + table.shape[1:], lambda i: (tick, 0, 0)))
    return pl.pallas_call(
        kernel,
        grid=(1,),
        out_shape=out_shape,
        in_specs=specs,
        out_specs=pl.BlockSpec(memory_space=pltpu.VMEM),
        compiler_params=pltpu.CompilerParams(vmem_limit_bytes=limit_mib * 1024 * 1024),
        cost_estimate=pl.CostEstimate(flops=flops, bytes_accessed=moved, transcendentals=0),
    )(*operands, *tables)


def choose_kernel(tokens, gain, first, second, out):
    half = out.shape[1]
    normed = rms_scale(tokens[...], gain[...]).astype(jnp.bfloat16).astype(jnp.float32)
    picked = matmul(first[0], normed[:, :half]) + matmul(second[0], normed[:, half:])
    out[...] = picked.astype(jnp.bfloat16)


def expert_kernel(tokens, w_gate, w_up, w_down, out):
    folded, half = tokens.shape
    slots = folded // 2
    place = lambda row: (row // 4) * 8 + row % 4
    first = matmul(one_hot(slots, folded, place), tokens[...]).astype(jnp.bfloat16)
    second = matmul(one_hot(slots, folded, lambda row: place(row) + 4), tokens[...])
    second = second.astype(jnp.bfloat16)
    gate_proj = matmul(first, w_gate[:half, :]) + matmul(second, w_gate[half:, :])
    up_proj = matmul(first, w_up[:half, :]) + matmul(second, w_up[half:, :])
    hidden = (gate_proj / (1.0 + jnp.exp(-gate_proj)) * up_proj).astype(jnp.bfloat16)
    width = 512
    for start in range(0, 2 * half, width):
        cols = slice(start, start + width)
        out[:, cols] = matmul(hidden, w_down[:, cols]).astype(jnp.bfloat16)


def total_kernel(parts, quarters, out):
    folded, half = out.shape
    slots = folded // 2
    total = quarters[:slots, :].astype(jnp.float32)
    for k in range(1, parts):
        total = total + quarters[k * slots : (k + 1) * slots, :].astype(jnp.float32)
    total = total.astype(jnp.bfloat16)
    place = lambda row: (row // 8) * 4 + row % 4
    first = one_hot(folded, slots, place, lambda row: row % 8 < 4)
    second = one_hot(folded, slots, place, lambda row: row % 8 >= 4)
    spread = matmul(first, total[:, :half]) + matmul(second, total[:, half:])
    out[...] = spread.astype(jnp.bfloat16)


def combine_kernel(tokens, returned, first, second, out):
    half = returned.shape[1]
    rows = returned[...].astype(jnp.float32)
    for weights, cols in ((first, slice(0, half)), (second, slice(half, 2 * half))):
        moe_sum = jnp.dot(
            weights[0],
            rows,
            precision=lax.Precision.HIGHEST,
            preferred_element_type=jnp.float32,
        )
        out[:, cols] = (tokens[:, cols].astype(jnp.float32) + moe_sum).astype(jnp.bfloat16)


def body(
    spans,
    attn_gain,
    kv_gain,
    moe_gain,
    w_latent,
    w_gate,
    w_up,
    w_down,
    expert_ids,
    gate_vals,
    owner_map,
    offsets,
):
    section_id = lax.axis_index("section")
    plane = lax.axis_index("z")
    column = lax.axis_index("y")
    n_planes = lax.axis_size("z")
    n_columns = lax.axis_size("y")
    member = plane * n_columns + column
    n_members = n_planes * n_columns
    n_sections = lax.axis_size("section")
    n_spans, span_dev, model_width = spans.shape
    kv_width = w_latent.shape[2]
    experts = n_members // EXP_SPLIT
    capacity = min(span_dev, 2 * span_dev * TOPK // experts)
    per_owner = span_dev // KVBLK
    all_experts = jnp.arange(experts, dtype=jnp.int32)
    local_gate = w_gate[0]
    local_up = w_up[0]
    local_down = w_down[0]
    latent_full = lax.all_gather(w_latent[0], ("z", "y"), axis=0, tiled=True)

    def by_tick(values):
        padded = jnp.concatenate([jnp.zeros_like(values), values], axis=0)
        return lax.dynamic_slice_in_dim(padded, n_spans - section_id, n_sections, 0)

    own_ids = by_tick(lax.dynamic_slice_in_dim(expert_ids[0], member * span_dev, span_dev, 1))
    gate_rows = by_tick(gate_vals[0])
    own_table = packing(own_ids, all_experts, capacity)
    gate_for = jnp.sum(
        jnp.where(
            own_ids[..., None] == all_experts[None, None, None, :], gate_rows[..., None], 0.0
        ),
        axis=2,
    )
    weighting = own_table.astype(jnp.float32) * jnp.transpose(gate_for, (0, 2, 1))[:, :, None, :]
    no_slot = jnp.zeros_like(weighting)

    def folded(first, second):
        return jnp.concatenate([first, second], axis=2).reshape(n_sections, -1, span_dev)

    chooses = own_table.astype(jnp.float32)
    choose_first, choose_second = folded(chooses, no_slot), folded(no_slot, chooses)
    weigh_first = jnp.transpose(folded(weighting, no_slot), (0, 2, 1))
    weigh_second = jnp.transpose(folded(no_slot, weighting), (0, 2, 1))
    positions = (
        by_tick(offsets)[:, None]
        + member * span_dev
        + jnp.arange(span_dev, dtype=jnp.int32)[None, :]
    )
    block_order = by_tick(owner_map[0])

    def project(first, last):
        rows = jnp.concatenate(tick_rows[first:last], axis=0)
        normed = rms_scale(rows, attn_gain[0]).astype(jnp.bfloat16)
        latent = jnp.dot(normed, latent_full, preferred_element_type=jnp.float32)
        return latent_rows(latent, kv_gain[0], positions[first:last].reshape(-1))

    def owned_rows(order):
        block = jnp.repeat(order, KVBLK, axis=-1)
        return block * KVBLK + jnp.arange(block.shape[-1], dtype=jnp.int32) % KVBLK

    def deliver_whole(kv_rows, first, last):
        count = last - first
        gathered = lax.all_gather(kv_rows, ("z", "y"), axis=0)
        gathered = gathered.reshape(n_members, count, span_dev, kv_width)
        order = lax.dynamic_slice_in_dim(
            block_order[first:last], member * per_owner, per_owner, 1
        )
        every = jnp.arange(n_members * span_dev, dtype=jnp.int32)
        pick = (owned_rows(order)[..., None] == every).astype(jnp.bfloat16)
        pick = pick.reshape(count, span_dev, n_members, span_dev)
        return jnp.einsum(
            "tdmr,mtrk->tdk", pick, gathered, preferred_element_type=jnp.float32
        ).astype(jnp.bfloat16)

    def side_by_side(rows):
        wide = [rows[..., i : i + 8, :] for i in range(0, rows.shape[-2], 8)]
        wide = jnp.concatenate(wide, axis=-1)
        spare = model_width // 2 - wide.shape[-1]
        return jnp.pad(wide, [(0, 0)] * (wide.ndim - 1) + [(0, spare)])

    def apart(wide, count):
        pieces = [wide[..., i * kv_width : (i + 1) * kv_width] for i in range(count)]
        return jnp.concatenate(pieces, axis=-2)

    def pack_late(column_rows, first, last):
        count = last - first
        order = block_order[first:last].reshape(count, n_planes, n_columns, per_owner)
        order = lax.dynamic_index_in_dim(order, column, 2, keepdims=False)
        wanted = jnp.transpose(owned_rows(order), (1, 0, 2))
        col = jnp.arange(n_columns, dtype=jnp.int32)[:, None, None]
        tick = jnp.arange(count, dtype=jnp.int32)[None, :, None]
        row = jnp.arange(span_dev, dtype=jnp.int32)[None, None, :]
        held = (plane * n_columns + col) * span_dev + row + 0 * tick
        same = tick + 0 * held == jnp.arange(count, dtype=jnp.int32)[:, None, None, None]
        hit = (wanted[..., None, None, None] == held) & same[:, None]
        hit = hit.reshape(n_planes * count * span_dev, -1).astype(jnp.bfloat16)
        source = column_rows.reshape(-1, kv_width)
        packed = matmul(hit, source).astype(jnp.bfloat16)
        return side_by_side(packed.reshape(n_planes, count * span_dev, kv_width))

    def unpack_late(arrived, first, last):
        count = last - first
        rows = jnp.sum(arrived.astype(jnp.float32), axis=0).astype(jnp.bfloat16)
        return apart(rows, count).reshape(count, span_dev, kv_width)

    half = model_width // 2
    slots = experts * capacity
    tick_rows = []
    layer_in = jnp.zeros((span_dev, model_width), jnp.bfloat16)
    early = None
    flops = 2 * 3 * n_columns * slots * model_width * local_gate.shape[1]
    for tick in range(n_sections):
        last_tick = tick + 1 == n_sections
        tokens = jnp.where(section_id == 0, spans[tick], layer_in)
        tick_rows.append(tokens)
        if tick == 0:
            held = (tokens, choose_first, choose_second, weigh_first, weigh_second)
            held = lax.optimization_barrier(held)
            tokens, choose_first, choose_second, weigh_first, weigh_second = held
        if tick == 2:
            tokens, latent_full = lax.optimization_barrier((tokens, latent_full))
        if tick == EARLY - 1:
            early_rows = project(0, EARLY)
            tokens, early_rows = lax.optimization_barrier((tokens, early_rows))
            early = deliver_whole(early_rows, 0, EARLY)
        chosen = in_vmem(
            choose_kernel,
            jax.ShapeDtypeStruct((2 * slots, half), jnp.bfloat16),
            (tokens, moe_gain),
            8,
            tick=tick,
            tables=(choose_first, choose_second),
        )
        arrived = lax.all_to_all(chosen, "z", split_axis=0, concat_axis=0, tiled=True)
        if last_tick:
            late_rows = side_by_side(project(EARLY, n_sections))
            arrived = jnp.concatenate([arrived, late_rows], axis=0)
        token_rows = lax.all_gather(arrived, "y", axis=0, tiled=True)
        if last_tick:
            token_rows = token_rows.reshape(n_columns, -1, half)
            late_rows = apart(token_rows[:, 2 * slots :], n_sections - EARLY)
            token_rows = token_rows[:, : 2 * slots].reshape(-1, half)
        parts = in_vmem(
            expert_kernel,
            jax.ShapeDtypeStruct((n_columns * slots, model_width), jnp.bfloat16),
            (token_rows, local_gate, local_up, local_down),
            24,
            flops,
        )
        quarters = lax.all_to_all(parts, "y", split_axis=0, concat_axis=0, tiled=True)
        summed = in_vmem(
            lambda *refs: total_kernel(n_columns, *refs),
            jax.ShapeDtypeStruct((2 * slots, half), jnp.bfloat16),
            (quarters,),
            12,
        )
        if last_tick:
            late = pack_late(late_rows, EARLY, n_sections)
            summed = jnp.concatenate([summed.reshape(n_planes, -1, half), late], axis=1)
            summed = summed.reshape(-1, half)
        returned = lax.all_to_all(summed, "z", split_axis=0, concat_axis=0, tiled=True)
        if last_tick:
            returned = returned.reshape(n_planes, -1, half)
            late = unpack_late(returned[:, -8:], EARLY, n_sections)
            returned = returned[:, :-8].reshape(-1, half)
        layer_out = in_vmem(
            combine_kernel,
            jax.ShapeDtypeStruct((span_dev, model_width), jnp.bfloat16),
            (tokens, returned),
            8,
            tick=tick,
            tables=(weigh_first, weigh_second),
        )
        if not last_tick:
            layer_in = shifted(layer_out, "section", 1)
    delivered = [early, late]
    blank = jnp.zeros((n_spans, span_dev, kv_width), jnp.bfloat16)
    kv_ticks = jnp.concatenate(delivered + [blank], axis=0)
    kv_store = lax.dynamic_slice_in_dim(kv_ticks, section_id, n_spans, 0)
    return (layer_out[None], kv_store[None])


def solution(mesh):
    n_members = mesh.shape["ep"]
    grid = Mesh(
        mesh.devices.reshape(mesh.shape["section"], n_members // EXP_SPLIT, EXP_SPLIT),
        ("section", "z", "y"),
    )
    ep = ("z", "y")
    in_specs = (
        P(None, ep, None),
        P("section", None),
        P("section", None),
        P("section", None),
        P("section", ep, None),
        P("section", None, ep),
        P("section", None, ep),
        P("section", ep, None),
        P("section", None, None, None),
        P("section", None, ep, None),
        P("section", None, None),
        P(),
    )
    out_specs = (P("section", ep, None), P("section", None, ep, None))
    return jax.shard_map(body, mesh=grid, in_specs=in_specs, out_specs=out_specs, check_vma=False)
```

```python
import jax
import jax.numpy as jnp
from jax import lax
from jax.experimental import pallas as pl
from jax.experimental.pallas import tpu as pltpu
from jax.sharding import Mesh, PartitionSpec as P

LAT = 512
EXP_SPLIT = 4
TOPK = 2
KVBLK = 4
EARLY = 7


eps = 1e-06


def shifted(block, axis, distance):
    devices = range(lax.axis_size(axis))
    route = [(i - distance, i) for i in devices if i - distance in devices]
    return lax.ppermute(block, axis, route)


def rms_scale(values, gain_vec):
    values = values.astype(jnp.float32)
    return values * lax.rsqrt(jnp.mean(values * values, axis=-1, keepdims=True) + eps) * gain_vec


def rotation(width, positions):
    half_dim = width // 2
    frequency = 10000.0 ** (-jnp.arange(half_dim, dtype=jnp.float32) / half_dim)
    angles = positions.astype(jnp.float32)[:, None] * frequency[None, :]
    return jnp.tile(jnp.cos(angles), (1, 2)), jnp.tile(jnp.sin(angles), (1, 2))


def one_hot(rows, cols, wanted, kept=None):
    row = lax.broadcasted_iota(jnp.int32, (rows, cols), 0)
    col = lax.broadcasted_iota(jnp.int32, (rows, cols), 1)
    hit = col == wanted(row)
    if kept is not None:
        hit = hit & kept(row)
    return jnp.where(hit, 1.0, 0.0).astype(jnp.bfloat16)


def matmul(left, right):
    return jnp.dot(left, right, preferred_element_type=jnp.float32)


def in_vmem(kernel, out_shape, operands, limit_mib, flops=0, tick=None, tables=()):
    moved = sum(x.size * x.dtype.itemsize for x in operands)
    specs = [pl.BlockSpec(memory_space=pltpu.VMEM)] * len(operands)
    for table in tables:
        specs.append(pl.BlockSpec((1,) + table.shape[1:], lambda i: (tick, 0, 0)))
    return pl.pallas_call(
        kernel,
        grid=(1,),
        out_shape=out_shape,
        in_specs=specs,
        out_specs=pl.BlockSpec(memory_space=pltpu.VMEM),
        compiler_params=pltpu.CompilerParams(vmem_limit_bytes=limit_mib * 1024 * 1024),
        cost_estimate=pl.CostEstimate(flops=flops, bytes_accessed=moved, transcendentals=0),
    )(*operands, *tables)


def slot_hits(routes, folded, offset):
    rows = routes.shape[0]
    line = lax.broadcasted_iota(jnp.int32, (rows, folded), 1)
    expert = (line // 8).astype(jnp.float32)
    slot = (line % 8 - offset).astype(jnp.float32)
    picked = jnp.zeros((rows, folded), jnp.float32)
    weight = jnp.zeros((rows, folded), jnp.float32)
    for k in range(TOPK):
        same = routes[:, k : k + 1] == expert
        picked = jnp.where(same, 1.0, picked)
        weight = jnp.where(same, routes[:, TOPK + k : TOPK + k + 1], weight)
    row = lax.broadcasted_iota(jnp.int32, (rows, rows), 0)
    col = lax.broadcasted_iota(jnp.int32, (rows, rows), 1)
    earlier = jnp.where(col < row, 1.0, 0.0)
    rank = matmul(earlier, picked)
    hit = (picked > 0.5) & (rank == slot) & (slot >= 0.0) & (slot < 4.0)
    return jnp.where(hit, 1.0, 0.0), jnp.where(hit, weight, 0.0)


def choose_kernel(tokens, gain, routes, out):
    folded, half = out.shape
    normed = rms_scale(tokens[...], gain[...]).astype(jnp.bfloat16).astype(jnp.float32)
    picked = 0.0
    for offset, part in ((0, normed[:, :half]), (4, normed[:, half:])):
        hits, _ = slot_hits(routes[0], folded, offset)
        picked = picked + lax.dot_general(
            hits, part, (((0,), (0,)), ((), ())), preferred_element_type=jnp.float32
        )
    out[...] = picked.astype(jnp.bfloat16)


def latent_kernel(rows, attn_gain, kv_gain, w_latent, cosine, sine, out):
    normed = rms_scale(rows[...], attn_gain[...]).astype(jnp.bfloat16)
    latent = matmul(normed, w_latent[...])
    out[:, :LAT] = rms_scale(latent[:, :LAT], kv_gain[...]).astype(jnp.bfloat16)
    tail = latent[:, LAT:]
    width = tail.shape[1]
    row = lax.broadcasted_iota(jnp.int32, (width, width), 0)
    col = lax.broadcasted_iota(jnp.int32, (width, width), 1)
    turn = jnp.where(row == col + width // 2, -1.0, jnp.where(row + width // 2 == col, 1.0, 0.0))
    turned = jnp.dot(
        tail, turn, precision=lax.Precision.HIGHEST, preferred_element_type=jnp.float32
    )
    out[:, LAT:] = (tail * cosine[...] + turned * sine[...]).astype(jnp.bfloat16)


def expert_kernel(columns, tokens, w_gate, w_up, w_down, out):
    height, half = tokens.shape
    slots = out.shape[0]
    each, stride = slots // columns, height // columns

    def place(row):
        within = row % each
        return (row // each) * stride + (within // 4) * 8 + within % 4

    first = matmul(one_hot(slots, height, place), tokens[...]).astype(jnp.bfloat16)
    second = matmul(one_hot(slots, height, lambda row: place(row) + 4), tokens[...])
    second = second.astype(jnp.bfloat16)
    gate_proj = matmul(first, w_gate[:half, :]) + matmul(second, w_gate[half:, :])
    up_proj = matmul(first, w_up[:half, :]) + matmul(second, w_up[half:, :])
    hidden = (gate_proj / (1.0 + jnp.exp(-gate_proj)) * up_proj).astype(jnp.bfloat16)
    width = 512
    for start in range(0, 2 * half, width):
        cols = slice(start, start + width)
        out[:, cols] = matmul(hidden, w_down[:, cols]).astype(jnp.bfloat16)


def total_kernel(parts, quarters, out):
    folded, half = out.shape
    slots = folded // 2
    total = quarters[:slots, :].astype(jnp.float32)
    for k in range(1, parts):
        total = total + quarters[k * slots : (k + 1) * slots, :].astype(jnp.float32)
    total = total.astype(jnp.bfloat16)
    place = lambda row: (row // 8) * 4 + row % 4
    first = one_hot(folded, slots, place, lambda row: row % 8 < 4)
    second = one_hot(folded, slots, place, lambda row: row % 8 >= 4)
    spread = matmul(first, total[:, :half]) + matmul(second, total[:, half:])
    out[...] = spread.astype(jnp.bfloat16)


def combine_kernel(tokens, returned, routes, out):
    folded, half = returned.shape
    rows = returned[...].astype(jnp.float32)
    for offset, cols in ((0, slice(0, half)), (4, slice(half, 2 * half))):
        _, weights = slot_hits(routes[0], folded, offset)
        moe_sum = jnp.dot(
            weights, rows, precision=lax.Precision.HIGHEST, preferred_element_type=jnp.float32
        )
        out[:, cols] = (tokens[:, cols].astype(jnp.float32) + moe_sum).astype(jnp.bfloat16)


def body(
    spans,
    attn_gain,
    kv_gain,
    moe_gain,
    w_latent,
    w_gate,
    w_up,
    w_down,
    expert_ids,
    gate_vals,
    owner_map,
    offsets,
):
    section_id = lax.axis_index("section")
    plane = lax.axis_index("z")
    column = lax.axis_index("y")
    n_planes = lax.axis_size("z")
    n_columns = lax.axis_size("y")
    member = plane * n_columns + column
    n_members = n_planes * n_columns
    n_sections = lax.axis_size("section")
    n_spans, span_dev, model_width = spans.shape
    kv_width = w_latent.shape[2]
    experts = n_members // EXP_SPLIT
    capacity = min(span_dev, 2 * span_dev * TOPK // experts)
    per_owner = span_dev // KVBLK
    local_gate = w_gate[0]
    local_up = w_up[0]
    local_down = w_down[0]
    latent_full = lax.all_gather(w_latent[0], ("z", "y"), axis=0, tiled=True)

    def by_tick(values):
        padded = jnp.concatenate([jnp.zeros_like(values), values], axis=0)
        return lax.dynamic_slice_in_dim(padded, n_spans - section_id, n_sections, 0)

    own_ids = by_tick(lax.dynamic_slice_in_dim(expert_ids[0], member * span_dev, span_dev, 1))
    routes = jnp.concatenate([own_ids.astype(jnp.float32), by_tick(gate_vals[0])], axis=2)

    def project(first, last, gains, weights, turns):
        rows = jnp.concatenate(tick_rows[first:last], axis=0)
        part = slice(first * span_dev, last * span_dev)
        return in_vmem(
            latent_kernel,
            jax.ShapeDtypeStruct((rows.shape[0], kv_width), jnp.bfloat16),
            (rows, *gains, weights, turns[0][part], turns[1][part]),
            16,
        )

    def owned_rows(order):
        block = jnp.repeat(order, KVBLK, axis=-1)
        return block * KVBLK + jnp.arange(block.shape[-1], dtype=jnp.int32) % KVBLK

    def deliver_whole(gathered, block_order, first, last):
        count = last - first
        gathered = gathered.reshape(n_members, count, span_dev, kv_width)
        order = lax.dynamic_slice_in_dim(
            block_order[first:last], member * per_owner, per_owner, 1
        )
        every = jnp.arange(n_members * span_dev, dtype=jnp.int32)
        pick = (owned_rows(order)[..., None] == every).astype(jnp.bfloat16)
        pick = pick.reshape(count, span_dev, n_members, span_dev)
        return jnp.einsum(
            "tdmr,mtrk->tdk", pick, gathered, preferred_element_type=jnp.float32
        ).astype(jnp.bfloat16)

    def side_by_side(rows):
        wide = [rows[..., i : i + 8, :] for i in range(0, rows.shape[-2], 8)]
        wide = jnp.concatenate(wide, axis=-1)
        spare = model_width // 2 - wide.shape[-1]
        return jnp.pad(wide, [(0, 0)] * (wide.ndim - 1) + [(0, spare)])

    def apart(wide, count):
        pieces = [wide[..., i * kv_width : (i + 1) * kv_width] for i in range(count)]
        return jnp.concatenate(pieces, axis=-2)

    def pack_late(column_rows, block_order, first, last):
        count = last - first
        order = block_order[first:last].reshape(count, n_planes, n_columns, per_owner)
        order = lax.dynamic_index_in_dim(order, column, 2, keepdims=False)
        wanted = jnp.transpose(owned_rows(order), (1, 0, 2))
        col = jnp.arange(n_columns, dtype=jnp.int32)[:, None, None]
        tick = jnp.arange(count, dtype=jnp.int32)[None, :, None]
        row = jnp.arange(span_dev, dtype=jnp.int32)[None, None, :]
        held = (plane * n_columns + col) * span_dev + row + 0 * tick
        same = tick + 0 * held == jnp.arange(count, dtype=jnp.int32)[:, None, None, None]
        hit = (wanted[..., None, None, None] == held) & same[:, None]
        hit = hit.reshape(n_planes * count * span_dev, -1).astype(jnp.bfloat16)
        source = column_rows.reshape(-1, kv_width)
        packed = matmul(hit, source).astype(jnp.bfloat16)
        return side_by_side(packed.reshape(n_planes, count * span_dev, kv_width))

    def unpack_late(arrived, first, last):
        count = last - first
        rows = jnp.sum(arrived.astype(jnp.float32), axis=0).astype(jnp.bfloat16)
        return apart(rows, count).reshape(count, span_dev, kv_width)

    half = model_width // 2
    slots = experts * capacity
    tick_rows = []
    layer_in = jnp.zeros((span_dev, model_width), jnp.bfloat16)
    gains = (attn_gain, kv_gain)
    flops = 2 * 3 * n_columns * slots * model_width * local_gate.shape[1]
    for tick in range(n_sections):
        last_tick = tick + 1 == n_sections
        tokens = jnp.where(section_id == 0, spans[tick], layer_in)
        tick_rows.append(tokens)
        if last_tick:
            late_rows = project(EARLY, n_sections, gains, latent_full, turns)
            tokens, late_rows = lax.optimization_barrier((tokens, late_rows))
        chosen = in_vmem(
            choose_kernel,
            jax.ShapeDtypeStruct((2 * slots, half), jnp.bfloat16),
            (tokens, moe_gain),
            8,
            tick=tick,
            tables=(routes,),
        )
        if tick == 0:
            chosen, offsets = lax.optimization_barrier((chosen, offsets))
            positions = by_tick(offsets)[:, None] + member * span_dev
            positions = positions + jnp.arange(span_dev, dtype=jnp.int32)[None, :]
            turns = rotation(kv_width - LAT, positions.reshape(-1))
        arrived = lax.all_to_all(chosen, "z", split_axis=0, concat_axis=0, tiled=True)
        if tick == 0:
            arrived, turns = lax.optimization_barrier((arrived, turns))
        if last_tick:
            arrived = jnp.concatenate([arrived, side_by_side(late_rows)], axis=0)
        token_rows = lax.all_gather(arrived, "y", axis=0, tiled=True)
        parts = in_vmem(
            lambda *refs: expert_kernel(n_columns, *refs),
            jax.ShapeDtypeStruct((n_columns * slots, model_width), jnp.bfloat16),
            (token_rows, local_gate, local_up, local_down),
            24,
            flops,
        )
        if tick == 1:
            parts, latent_full = lax.optimization_barrier((parts, latent_full))
        if tick == EARLY - 1:
            held = lax.optimization_barrier((parts, tick_rows, gains, latent_full, turns))
            parts, tick_rows, gains, latent_full, turns = held
            early_rows = project(0, EARLY, gains, latent_full, turns)
            parts, early_rows = lax.optimization_barrier((parts, early_rows))
            early = lax.all_gather(early_rows, ("z", "y"), axis=0)
        if last_tick:
            held = (parts, token_rows, owner_map)
            parts, token_rows, owner_map = lax.optimization_barrier(held)
            block_order = by_tick(owner_map[0])
        quarters = lax.all_to_all(parts, "y", split_axis=0, concat_axis=0, tiled=True)
        summed = in_vmem(
            lambda *refs: total_kernel(n_columns, *refs),
            jax.ShapeDtypeStruct((2 * slots, half), jnp.bfloat16),
            (quarters,),
            12,
        )
        if last_tick:
            late_rows = token_rows.reshape(n_columns, -1, half)[:, 2 * slots :]
            late_rows = apart(late_rows, n_sections - EARLY)
            late = pack_late(late_rows, block_order, EARLY, n_sections)
            summed = jnp.concatenate([summed.reshape(n_planes, -1, half), late], axis=1)
            summed = summed.reshape(-1, half)
        returned = lax.all_to_all(summed, "z", split_axis=0, concat_axis=0, tiled=True)
        if last_tick:
            returned = returned.reshape(n_planes, -1, half)
            late = unpack_late(returned[:, -8:], EARLY, n_sections)
            returned = returned[:, :-8].reshape(-1, half)
        layer_out = in_vmem(
            combine_kernel,
            jax.ShapeDtypeStruct((span_dev, model_width), jnp.bfloat16),
            (tokens, returned),
            8,
            tick=tick,
            tables=(routes,),
        )
        if not last_tick:
            layer_in = shifted(layer_out, "section", 1)
    early = deliver_whole(early, block_order, 0, EARLY)
    delivered = [early, late]
    blank = jnp.zeros((n_spans, span_dev, kv_width), jnp.bfloat16)
    kv_ticks = jnp.concatenate(delivered + [blank], axis=0)
    kv_store = lax.dynamic_slice_in_dim(kv_ticks, section_id, n_spans, 0)
    return (layer_out[None], kv_store[None])


def solution(mesh):
    n_members = mesh.shape["ep"]
    grid = Mesh(
        mesh.devices.reshape(mesh.shape["section"], n_members // EXP_SPLIT, EXP_SPLIT),
        ("section", "z", "y"),
    )
    ep = ("z", "y")
    in_specs = (
        P(None, ep, None),
        P("section", None),
        P("section", None),
        P("section", None),
        P("section", ep, None),
        P("section", None, ep),
        P("section", None, ep),
        P("section", ep, None),
        P("section", None, None, None),
        P("section", None, ep, None),
        P("section", None, None),
        P(),
    )
    out_specs = (P("section", ep, None), P("section", None, ep, None))
    return jax.shard_map(body, mesh=grid, in_specs=in_specs, out_specs=out_specs, check_vma=False)
```

```python
import jax
import jax.numpy as jnp
import numpy as np
from jax import lax
from jax.experimental import pallas as pl
from jax.experimental.pallas import tpu as pltpu
from jax.sharding import Mesh, PartitionSpec as P

LAT = 512
EXP_SPLIT = 4
TOPK = 2
KVBLK = 4
EARLY = 7


eps = 1e-06


def shifted(block, axis, distance):
    devices = range(lax.axis_size(axis))
    route = [(i - distance, i) for i in devices if i - distance in devices]
    return lax.ppermute(block, axis, route)


def rms_scale(values, gain_vec):
    values = values.astype(jnp.float32)
    return values * lax.rsqrt(jnp.mean(values * values, axis=-1, keepdims=True) + eps) * gain_vec


def rotation(width, positions):
    half_dim = width // 2
    frequency = 10000.0 ** (-jnp.arange(half_dim, dtype=jnp.float32) / half_dim)
    angles = positions.astype(jnp.float32)[:, None] * frequency[None, :]
    return jnp.tile(jnp.cos(angles), (1, 2)), jnp.tile(jnp.sin(angles), (1, 2))


def one_hot(rows, cols, wanted, kept=None):
    row = lax.broadcasted_iota(jnp.int32, (rows, cols), 0)
    col = lax.broadcasted_iota(jnp.int32, (rows, cols), 1)
    hit = col == wanted(row)
    if kept is not None:
        hit = hit & kept(row)
    return jnp.where(hit, 1.0, 0.0).astype(jnp.bfloat16)


def matmul(left, right):
    return jnp.dot(left, right, preferred_element_type=jnp.float32)


def in_vmem(kernel, out_shape, operands, limit_mib, flops=0, tick=None, tables=()):
    moved = sum(x.size * x.dtype.itemsize for x in operands)
    specs = [pl.BlockSpec(memory_space=pltpu.VMEM)] * len(operands)
    for table in tables:
        specs.append(pl.BlockSpec((1,) + table.shape[1:], lambda i: (tick, 0, 0)))
    return pl.pallas_call(
        kernel,
        grid=(1,),
        out_shape=out_shape,
        in_specs=specs,
        out_specs=pl.BlockSpec(memory_space=pltpu.VMEM),
        compiler_params=pltpu.CompilerParams(vmem_limit_bytes=limit_mib * 1024 * 1024),
        cost_estimate=pl.CostEstimate(flops=flops, bytes_accessed=moved, transcendentals=0),
    )(*operands, *tables)


def slot_hits(routes, folded, offset):
    rows = routes.shape[0]
    line = lax.broadcasted_iota(jnp.int32, (rows, folded), 1)
    expert = (line // 8).astype(jnp.float32)
    slot = (line % 8 - offset).astype(jnp.float32)
    picked = jnp.zeros((rows, folded), jnp.float32)
    weight = jnp.zeros((rows, folded), jnp.float32)
    for k in range(TOPK):
        same = routes[:, k : k + 1] == expert
        picked = jnp.where(same, 1.0, picked)
        weight = jnp.where(same, routes[:, TOPK + k : TOPK + k + 1], weight)
    row = lax.broadcasted_iota(jnp.int32, (rows, rows), 0)
    col = lax.broadcasted_iota(jnp.int32, (rows, rows), 1)
    earlier = jnp.where(col < row, 1.0, 0.0)
    rank = matmul(earlier, picked)
    hit = (picked > 0.5) & (rank == slot) & (slot >= 0.0) & (slot < 4.0)
    return jnp.where(hit, 1.0, 0.0), jnp.where(hit, weight, 0.0)


def choose_kernel(tokens, gain, routes, out):
    folded, half = out.shape
    normed = rms_scale(tokens[...], gain[...]).astype(jnp.bfloat16).astype(jnp.float32)
    picked = 0.0
    for offset, part in ((0, normed[:, :half]), (4, normed[:, half:])):
        hits, _ = slot_hits(routes[0], folded, offset)
        picked = picked + lax.dot_general(
            hits, part, (((0,), (0,)), ((), ())), preferred_element_type=jnp.float32
        )
    out[...] = picked.astype(jnp.bfloat16)


def latent_kernel(rows, attn_gain, kv_gain, w_latent, cosine, sine, out):
    normed = rms_scale(rows[...], attn_gain[...]).astype(jnp.bfloat16)
    latent = matmul(normed, w_latent[...])
    out[:, :LAT] = rms_scale(latent[:, :LAT], kv_gain[...]).astype(jnp.bfloat16)
    tail = latent[:, LAT:]
    width = tail.shape[1]
    row = lax.broadcasted_iota(jnp.int32, (width, width), 0)
    col = lax.broadcasted_iota(jnp.int32, (width, width), 1)
    turn = jnp.where(row == col + width // 2, -1.0, jnp.where(row + width // 2 == col, 1.0, 0.0))
    turned = jnp.dot(
        tail, turn, precision=lax.Precision.HIGHEST, preferred_element_type=jnp.float32
    )
    out[:, LAT:] = (tail * cosine[...] + turned * sine[...]).astype(jnp.bfloat16)


def expert_kernel(columns, tokens, w_gate, w_up, w_down, out):
    height, half = tokens.shape
    slots = out.shape[0]
    each, stride = slots // columns, height // columns

    def place(row):
        within = row % each
        return (row // each) * stride + (within // 4) * 8 + within % 4

    first = matmul(one_hot(slots, height, place), tokens[...]).astype(jnp.bfloat16)
    second = matmul(one_hot(slots, height, lambda row: place(row) + 4), tokens[...])
    second = second.astype(jnp.bfloat16)
    gate_proj = matmul(first, w_gate[:half, :]) + matmul(second, w_gate[half:, :])
    up_proj = matmul(first, w_up[:half, :]) + matmul(second, w_up[half:, :])
    hidden = (gate_proj / (1.0 + jnp.exp(-gate_proj)) * up_proj).astype(jnp.bfloat16)
    width = 512
    for start in range(0, 2 * half, width):
        cols = slice(start, start + width)
        out[:, cols] = matmul(hidden, w_down[:, cols]).astype(jnp.bfloat16)


def total_kernel(parts, quarters, out):
    folded, half = out.shape
    slots = folded // 2
    total = quarters[:slots, :].astype(jnp.float32)
    for k in range(1, parts):
        total = total + quarters[k * slots : (k + 1) * slots, :].astype(jnp.float32)
    total = total.astype(jnp.bfloat16)
    place = lambda row: (row // 8) * 4 + row % 4
    first = one_hot(folded, slots, place, lambda row: row % 8 < 4)
    second = one_hot(folded, slots, place, lambda row: row % 8 >= 4)
    spread = matmul(first, total[:, :half]) + matmul(second, total[:, half:])
    out[...] = spread.astype(jnp.bfloat16)


def combine_kernel(tokens, returned, routes, out):
    folded, half = returned.shape
    rows = returned[...].astype(jnp.float32)
    for offset, cols in ((0, slice(0, half)), (4, slice(half, 2 * half))):
        _, weights = slot_hits(routes[0], folded, offset)
        moe_sum = jnp.dot(
            weights, rows, precision=lax.Precision.HIGHEST, preferred_element_type=jnp.float32
        )
        out[:, cols] = (tokens[:, cols].astype(jnp.float32) + moe_sum).astype(jnp.bfloat16)


def body(
    spans,
    attn_gain,
    kv_gain,
    moe_gain,
    w_latent,
    w_gate,
    w_up,
    w_down,
    expert_ids,
    gate_vals,
    owner_map,
    offsets,
):
    section_id = lax.axis_index("section")
    plane = lax.axis_index("z")
    column = lax.axis_index("y")
    n_planes = lax.axis_size("z")
    n_columns = lax.axis_size("y")
    member = plane * n_columns + column
    n_members = n_planes * n_columns
    n_sections = lax.axis_size("section")
    n_spans, span_dev, model_width = spans.shape
    kv_width = w_latent.shape[2]
    experts = n_members // EXP_SPLIT
    capacity = min(span_dev, 2 * span_dev * TOPK // experts)
    per_owner = span_dev // KVBLK
    local_gate = w_gate[0]
    local_up = w_up[0]
    local_down = w_down[0]
    latent_full = lax.all_gather(w_latent[0], ("z", "y"), axis=0, tiled=True)

    def by_tick(values):
        padded = jnp.concatenate([jnp.zeros_like(values), values], axis=0)
        return lax.dynamic_slice_in_dim(padded, n_spans - section_id, n_sections, 0)

    own_ids = by_tick(lax.dynamic_slice_in_dim(expert_ids[0], member * span_dev, span_dev, 1))
    routes = jnp.concatenate([own_ids.astype(jnp.float32), by_tick(gate_vals[0])], axis=2)

    def project(first, last, gains, weights, turns):
        rows = jnp.concatenate(tick_rows[first:last], axis=0)
        part = slice(first * span_dev, last * span_dev)
        return in_vmem(
            latent_kernel,
            jax.ShapeDtypeStruct((rows.shape[0], kv_width), jnp.bfloat16),
            (rows, *gains, weights, turns[0][part], turns[1][part]),
            16,
        )

    def owned_rows(order):
        block = jnp.repeat(order, KVBLK, axis=-1)
        return block * KVBLK + np.arange(block.shape[-1], dtype=np.int32) % KVBLK

    def deliver_whole(gathered, block_order, first, last):
        count = last - first
        gathered = gathered.reshape(n_members, count, span_dev, kv_width)
        order = lax.dynamic_slice_in_dim(
            block_order[first:last], member * per_owner, per_owner, 1
        )
        every = np.arange(n_members * span_dev, dtype=np.int32)
        pick = (owned_rows(order)[..., None] == every).astype(jnp.bfloat16)
        pick = pick.reshape(count, span_dev, n_members, span_dev)
        return jnp.einsum(
            "tdmr,mtrk->tdk", pick, gathered, preferred_element_type=jnp.float32
        ).astype(jnp.bfloat16)

    def side_by_side(rows):
        wide = [rows[..., i : i + 8, :] for i in range(0, rows.shape[-2], 8)]
        wide = jnp.concatenate(wide, axis=-1)
        spare = model_width // 2 - wide.shape[-1]
        return jnp.pad(wide, [(0, 0)] * (wide.ndim - 1) + [(0, spare)])

    def apart(wide, count):
        pieces = [wide[..., i * kv_width : (i + 1) * kv_width] for i in range(count)]
        return jnp.concatenate(pieces, axis=-2)

    def pack_late(column_rows, block_order, first, last):
        count = last - first
        order = block_order[first:last].reshape(count, n_planes, n_columns, per_owner)
        order = lax.dynamic_index_in_dim(order, column, 2, keepdims=False)
        wanted = jnp.transpose(owned_rows(order), (1, 0, 2))
        col = np.arange(n_columns, dtype=np.int32)[:, None, None]
        tick = np.arange(count, dtype=np.int32)[None, :, None]
        row = np.arange(span_dev, dtype=np.int32)[None, None, :]
        held = (plane * n_columns + col) * span_dev + row + 0 * tick
        same = tick + 0 * held == np.arange(count, dtype=np.int32)[:, None, None, None]
        hit = (wanted[..., None, None, None] == held) & same[:, None]
        hit = hit.reshape(n_planes * count * span_dev, -1).astype(jnp.bfloat16)
        source = column_rows.reshape(-1, kv_width)
        packed = matmul(hit, source).astype(jnp.bfloat16)
        return side_by_side(packed.reshape(n_planes, count * span_dev, kv_width))

    def unpack_late(arrived, first, last):
        count = last - first
        rows = jnp.sum(arrived.astype(jnp.float32), axis=0).astype(jnp.bfloat16)
        return apart(rows, count).reshape(count, span_dev, kv_width)

    half = model_width // 2
    slots = experts * capacity
    tick_rows = []
    layer_in = jnp.zeros((span_dev, model_width), jnp.bfloat16)
    gains = (attn_gain, kv_gain)
    flops = 2 * 3 * n_columns * slots * model_width * local_gate.shape[1]
    for tick in range(n_sections):
        last_tick = tick + 1 == n_sections
        tokens = jnp.where(section_id == 0, spans[tick], layer_in)
        tick_rows.append(tokens)
        if last_tick:
            late_rows = side_by_side(project(EARLY, n_sections, gains, latent_full, turns))
            tokens, late_rows = lax.optimization_barrier((tokens, late_rows))
        chosen = in_vmem(
            choose_kernel,
            jax.ShapeDtypeStruct((2 * slots, half), jnp.bfloat16),
            (tokens, moe_gain),
            8,
            tick=tick,
            tables=(routes,),
        )
        if tick == 0:
            chosen, offsets = lax.optimization_barrier((chosen, offsets))
            positions = by_tick(offsets)[:, None] + member * span_dev
            positions = positions + jnp.arange(span_dev, dtype=jnp.int32)[None, :]
            turns = rotation(kv_width - LAT, positions.reshape(-1))
        arrived = lax.all_to_all(chosen, "z", split_axis=0, concat_axis=0, tiled=True)
        if last_tick:
            arrived = jnp.concatenate([arrived, late_rows], axis=0)
        if tick == 0:
            arrived, turns = lax.optimization_barrier((arrived, turns))
        token_rows = lax.all_gather(arrived, "y", axis=0, tiled=True)
        parts = in_vmem(
            lambda *refs: expert_kernel(n_columns, *refs),
            jax.ShapeDtypeStruct((n_columns * slots, model_width), jnp.bfloat16),
            (token_rows, local_gate, local_up, local_down),
            24,
            flops,
        )
        if tick == 1:
            parts, latent_full = lax.optimization_barrier((parts, latent_full))
        if tick == EARLY - 1:
            held = lax.optimization_barrier((parts, tick_rows, gains, latent_full, turns))
            parts, tick_rows, gains, latent_full, turns = held
            early_rows = project(0, EARLY, gains, latent_full, turns)
            parts, early_rows = lax.optimization_barrier((parts, early_rows))
            early = lax.all_gather(early_rows, ("z", "y"), axis=0)
        if last_tick:
            held = (parts, token_rows, owner_map)
            parts, token_rows, owner_map = lax.optimization_barrier(held)
            block_order = by_tick(owner_map[0])
        quarters = lax.all_to_all(parts, "y", split_axis=0, concat_axis=0, tiled=True)
        if last_tick:
            quarters, early = lax.optimization_barrier((quarters, early))
        summed = in_vmem(
            lambda *refs: total_kernel(n_columns, *refs),
            jax.ShapeDtypeStruct((2 * slots, half), jnp.bfloat16),
            (quarters,),
            12,
        )
        if last_tick:
            late_rows = token_rows.reshape(n_columns, -1, half)[:, 2 * slots :]
            late_rows = apart(late_rows, n_sections - EARLY)
            late = pack_late(late_rows, block_order, EARLY, n_sections)
            summed = jnp.concatenate([summed.reshape(n_planes, -1, half), late], axis=1)
            summed = summed.reshape(-1, half)
        returned = lax.all_to_all(summed, "z", split_axis=0, concat_axis=0, tiled=True)
        if last_tick:
            returned = returned.reshape(n_planes, -1, half)
            late = unpack_late(returned[:, -8:], EARLY, n_sections)
            returned = returned[:, :-8].reshape(-1, half)
        layer_out = in_vmem(
            combine_kernel,
            jax.ShapeDtypeStruct((span_dev, model_width), jnp.bfloat16),
            (tokens, returned),
            8,
            tick=tick,
            tables=(routes,),
        )
        if not last_tick:
            layer_in = shifted(layer_out, "section", 1)
    early = deliver_whole(early, block_order, 0, EARLY)
    delivered = [early, late]
    blank = jnp.zeros((n_spans, span_dev, kv_width), jnp.bfloat16)
    kv_ticks = jnp.concatenate(delivered + [blank], axis=0)
    kv_store = lax.dynamic_slice_in_dim(kv_ticks, section_id, n_spans, 0)
    return (layer_out[None], kv_store[None])


def solution(mesh):
    n_members = mesh.shape["ep"]
    grid = Mesh(
        mesh.devices.reshape(mesh.shape["section"], n_members // EXP_SPLIT, EXP_SPLIT),
        ("section", "z", "y"),
    )
    ep = ("z", "y")
    in_specs = (
        P(None, ep, None),
        P("section", None),
        P("section", None),
        P("section", None),
        P("section", ep, None),
        P("section", None, ep),
        P("section", None, ep),
        P("section", ep, None),
        P("section", None, None, None),
        P("section", None, ep, None),
        P("section", None, None),
        P(),
    )
    out_specs = (P("section", ep, None), P("section", None, ep, None))
    return jax.shard_map(body, mesh=grid, in_specs=in_specs, out_specs=out_specs, check_vma=False)
```

```python
import functools

import jax
import jax.numpy as jnp
import numpy as np
from jax import lax
from jax.experimental import pallas as pl
from jax.experimental.pallas import tpu as pltpu
from jax.sharding import Mesh, PartitionSpec as P

LAT = 512
EXP_SPLIT = 4
TOPK = 2
KVBLK = 4
EARLY = 7


eps = 1e-06


def shifted(block, axis, distance):
    devices = range(lax.axis_size(axis))
    route = [(i - distance, i) for i in devices if i - distance in devices]
    return lax.ppermute(block, axis, route)


def rms_scale(values, gain_vec):
    values = values.astype(jnp.float32)
    return values * lax.rsqrt(jnp.mean(values * values, axis=-1, keepdims=True) + eps) * gain_vec


def rotation(width, positions):
    half_dim = width // 2
    frequency = 10000.0 ** (-jnp.arange(half_dim, dtype=jnp.float32) / half_dim)
    angles = positions.astype(jnp.float32)[:, None] * frequency[None, :]
    return jnp.tile(jnp.cos(angles), (1, 2)), jnp.tile(jnp.sin(angles), (1, 2))


def one_hot(rows, cols, wanted, kept=None):
    row = lax.broadcasted_iota(jnp.int32, (rows, cols), 0)
    col = lax.broadcasted_iota(jnp.int32, (rows, cols), 1)
    hit = col == wanted(row)
    if kept is not None:
        hit = hit & kept(row)
    return jnp.where(hit, 1.0, 0.0).astype(jnp.bfloat16)


def matmul(left, right):
    return jnp.dot(left, right, preferred_element_type=jnp.float32)


def in_vmem(kernel, out_shape, operands, limit_mib, flops=0, tick=None, tables=()):
    moved = sum(x.size * x.dtype.itemsize for x in operands)
    specs = [pl.BlockSpec(memory_space=pltpu.VMEM)] * len(operands)
    for table in tables:
        specs.append(pl.BlockSpec((1,) + table.shape[1:], lambda i: (tick, 0, 0)))
    return pl.pallas_call(
        kernel,
        grid=(1,),
        out_shape=out_shape,
        in_specs=specs,
        out_specs=jax.tree.map(lambda _: pl.BlockSpec(memory_space=pltpu.VMEM), out_shape),
        compiler_params=pltpu.CompilerParams(vmem_limit_bytes=limit_mib * 1024 * 1024),
        cost_estimate=pl.CostEstimate(flops=flops, bytes_accessed=moved, transcendentals=0),
    )(*operands, *tables)


def slot_hits(routes, folded, offset):
    rows = routes.shape[0]
    line = lax.broadcasted_iota(jnp.int32, (rows, folded), 1)
    expert = (line // 8).astype(jnp.float32)
    slot = (line % 8 - offset).astype(jnp.float32)
    picked = jnp.zeros((rows, folded), jnp.float32)
    weight = jnp.zeros((rows, folded), jnp.float32)
    for k in range(TOPK):
        same = routes[:, k : k + 1] == expert
        picked = jnp.where(same, 1.0, picked)
        weight = jnp.where(same, routes[:, TOPK + k : TOPK + k + 1], weight)
    row = lax.broadcasted_iota(jnp.int32, (rows, rows), 0)
    col = lax.broadcasted_iota(jnp.int32, (rows, rows), 1)
    earlier = jnp.where(col < row, 1.0, 0.0)
    rank = matmul(earlier, picked)
    hit = (picked > 0.5) & (rank == slot) & (slot >= 0.0) & (slot < 4.0)
    return jnp.where(hit, 1.0, 0.0), jnp.where(hit, weight, 0.0)


def table_kernel(folded, routes, hits_out, weights_out):
    for tick in range(routes.shape[0]):
        for k, offset in enumerate((0, 4)):
            hits, weights = slot_hits(routes[tick], folded, offset)
            cols = slice(k * folded, (k + 1) * folded)
            hits_out[tick, :, cols] = hits
            weights_out[tick, :, cols] = weights


def choose_kernel(made, tokens, gain, table, out):
    folded, half = out.shape
    normed = rms_scale(tokens[...], gain[...]).astype(jnp.bfloat16).astype(jnp.float32)
    picked = 0.0
    for k, offset in enumerate((0, 4)):
        if made:
            hits = table[0, :, k * folded : (k + 1) * folded]
        else:
            hits, _ = slot_hits(table[0], folded, offset)
        picked = picked + lax.dot_general(
            hits,
            normed[:, k * half : (k + 1) * half],
            (((0,), (0,)), ((), ())),
            preferred_element_type=jnp.float32,
        )
    out[...] = picked.astype(jnp.bfloat16)


def copies_kernel(rows, out):
    height = rows.shape[0]
    for k in range(out.shape[0] // height):
        out[k * height : (k + 1) * height, :] = rows[...]


def latent_kernel(rows, attn_gain, kv_gain, w_latent, cosine, sine, out):
    normed = rms_scale(rows[...], attn_gain[...]).astype(jnp.bfloat16)
    latent = matmul(normed, w_latent[...])
    out[:, :LAT] = rms_scale(latent[:, :LAT], kv_gain[...]).astype(jnp.bfloat16)
    tail = latent[:, LAT:]
    width = tail.shape[1]
    row = lax.broadcasted_iota(jnp.int32, (width, width), 0)
    col = lax.broadcasted_iota(jnp.int32, (width, width), 1)
    turn = jnp.where(row == col + width // 2, -1.0, jnp.where(row + width // 2 == col, 1.0, 0.0))
    turned = jnp.dot(
        tail, turn, precision=lax.Precision.HIGHEST, preferred_element_type=jnp.float32
    )
    out[:, LAT:] = (tail * cosine[...] + turned * sine[...]).astype(jnp.bfloat16)


def expert_kernel(columns, tokens, w_gate, w_up, w_down, out):
    height, half = tokens.shape
    slots = out.shape[0]
    each, stride = slots // columns, height // columns

    def place(row):
        within = row % each
        return (row // each) * stride + (within // 4) * 8 + within % 4

    first = matmul(one_hot(slots, height, place), tokens[...]).astype(jnp.bfloat16)
    second = matmul(one_hot(slots, height, lambda row: place(row) + 4), tokens[...])
    second = second.astype(jnp.bfloat16)
    gate_proj = matmul(first, w_gate[:half, :]) + matmul(second, w_gate[half:, :])
    up_proj = matmul(first, w_up[:half, :]) + matmul(second, w_up[half:, :])
    hidden = (gate_proj / (1.0 + jnp.exp(-gate_proj)) * up_proj).astype(jnp.bfloat16)
    width = 512
    for start in range(0, 2 * half, width):
        cols = slice(start, start + width)
        out[:, cols] = matmul(hidden, w_down[:, cols]).astype(jnp.bfloat16)


def total_kernel(parts, quarters, out):
    folded, half = out.shape
    slots = folded // 2
    total = quarters[:slots, :].astype(jnp.float32)
    for k in range(1, parts):
        total = total + quarters[k * slots : (k + 1) * slots, :].astype(jnp.float32)
    total = total.astype(jnp.bfloat16)
    place = lambda row: (row // 8) * 4 + row % 4
    first = one_hot(folded, slots, place, lambda row: row % 8 < 4)
    second = one_hot(folded, slots, place, lambda row: row % 8 >= 4)
    spread = matmul(first, total[:, :half]) + matmul(second, total[:, half:])
    out[...] = spread.astype(jnp.bfloat16)


def combine_kernel(tokens, returned, table, out):
    folded, half = returned.shape
    span_dev = tokens.shape[0]
    for k in range(2):
        cols = slice(k * half, (k + 1) * half)
        rest = table[0, :, k * folded : (k + 1) * folded]
        terms = []
        for _ in range(3):
            term = rest.astype(jnp.bfloat16)
            rest = rest - term.astype(jnp.float32)
            terms.append(term.astype(jnp.float32))
        terms = jnp.concatenate(terms, axis=0).astype(jnp.bfloat16)
        sums = matmul(terms, returned[...])
        moe_sum = sums[:span_dev] + sums[span_dev : 2 * span_dev] + sums[2 * span_dev :]
        out[:, cols] = (tokens[:, cols].astype(jnp.float32) + moe_sum).astype(jnp.bfloat16)


def body(
    spans,
    attn_gain,
    kv_gain,
    moe_gain,
    w_latent,
    w_gate,
    w_up,
    w_down,
    expert_ids,
    gate_vals,
    owner_map,
    offsets,
):
    section_id = lax.axis_index("section")
    plane = lax.axis_index("z")
    column = lax.axis_index("y")
    n_planes = lax.axis_size("z")
    n_columns = lax.axis_size("y")
    member = plane * n_columns + column
    n_members = n_planes * n_columns
    n_sections = lax.axis_size("section")
    n_spans, span_dev, model_width = spans.shape
    kv_width = w_latent.shape[2]
    experts = n_members // EXP_SPLIT
    capacity = min(span_dev, 2 * span_dev * TOPK // experts)
    per_owner = span_dev // KVBLK
    local_gate = w_gate[0]
    local_up = w_up[0]
    local_down = w_down[0]
    latent_full = lax.all_gather(w_latent[0], ("z", "y"), axis=0, tiled=True)

    def by_tick(values):
        padded = jnp.concatenate([jnp.zeros_like(values), values], axis=0)
        return lax.dynamic_slice_in_dim(padded, n_spans - section_id, n_sections, 0)

    own_ids = by_tick(lax.dynamic_slice_in_dim(expert_ids[0], member * span_dev, span_dev, 1))
    routes = jnp.concatenate([own_ids.astype(jnp.float32), by_tick(gate_vals[0])], axis=2)

    def project(first, last, gains, weights, turns):
        rows = jnp.concatenate(tick_rows[first:last], axis=0)
        part = slice(first * span_dev, last * span_dev)
        return in_vmem(
            latent_kernel,
            jax.ShapeDtypeStruct((rows.shape[0], kv_width), jnp.bfloat16),
            (rows, *gains, weights, turns[0][part], turns[1][part]),
            16,
        )

    def owned_rows(order):
        block = jnp.repeat(order, KVBLK, axis=-1)
        return block * KVBLK + np.arange(block.shape[-1], dtype=np.int32) % KVBLK

    def deliver_whole(gathered, block_order, first, last):
        count = last - first
        gathered = gathered.reshape(n_members, count, span_dev, kv_width)
        order = lax.dynamic_slice_in_dim(
            block_order[first:last], member * per_owner, per_owner, 1
        )
        every = np.arange(n_members * span_dev, dtype=np.int32)
        pick = (owned_rows(order)[..., None] == every).astype(jnp.bfloat16)
        pick = pick.reshape(count, span_dev, n_members, span_dev)
        return jnp.einsum(
            "tdmr,mtrk->tdk", pick, gathered, preferred_element_type=jnp.float32
        ).astype(jnp.bfloat16)

    def side_by_side(rows):
        wide = [rows[..., i : i + 8, :] for i in range(0, rows.shape[-2], 8)]
        wide = jnp.concatenate(wide, axis=-1)
        spare = model_width // 2 - wide.shape[-1]
        return jnp.pad(wide, [(0, 0)] * (wide.ndim - 1) + [(0, spare)])

    def apart(wide, count):
        pieces = [wide[..., i * kv_width : (i + 1) * kv_width] for i in range(count)]
        return jnp.concatenate(pieces, axis=-2)

    def pack_late(column_rows, block_order, first, last):
        count = last - first
        order = block_order[first:last].reshape(count, n_planes, n_columns, per_owner)
        order = lax.dynamic_index_in_dim(order, column, 2, keepdims=False)
        wanted = jnp.transpose(owned_rows(order), (1, 0, 2))
        col = np.arange(n_columns, dtype=np.int32)[:, None, None]
        tick = np.arange(count, dtype=np.int32)[None, :, None]
        row = np.arange(span_dev, dtype=np.int32)[None, None, :]
        held = (plane * n_columns + col) * span_dev + row + 0 * tick
        same = tick + 0 * held == np.arange(count, dtype=np.int32)[:, None, None, None]
        hit = (wanted[..., None, None, None] == held) & same[:, None]
        hit = hit.reshape(n_planes * count * span_dev, -1).astype(jnp.bfloat16)
        source = column_rows.reshape(-1, kv_width)
        packed = matmul(hit, source).astype(jnp.bfloat16)
        return side_by_side(packed.reshape(n_planes, count * span_dev, kv_width))

    def unpack_late(arrived, first, last):
        count = last - first
        rows = jnp.sum(arrived.astype(jnp.float32), axis=0).astype(jnp.bfloat16)
        return apart(rows, count).reshape(count, span_dev, kv_width)

    half = model_width // 2
    slots = experts * capacity
    tick_rows = []
    layer_in = jnp.zeros((span_dev, model_width), jnp.bfloat16)
    gains = (attn_gain, kv_gain)
    flops = 2 * 3 * n_columns * slots * model_width * local_gate.shape[1]
    for tick in range(n_sections):
        last_tick = tick + 1 == n_sections
        tokens = jnp.where(section_id == 0, spans[tick], layer_in)
        tick_rows.append(tokens)
        if last_tick:
            late_rows = side_by_side(project(EARLY, n_sections, gains, latent_full, turns))
            tokens, late_rows = lax.optimization_barrier((tokens, late_rows))
        chosen = in_vmem(
            functools.partial(choose_kernel, tick > 0),
            jax.ShapeDtypeStruct((2 * slots, half), jnp.bfloat16),
            (tokens, moe_gain),
            8,
            tick=tick,
            tables=(hits if tick else routes,),
        )
        if tick == 0:
            held = lax.optimization_barrier((chosen, offsets, routes))
            chosen, offsets, routes = held
            table = jax.ShapeDtypeStruct((n_sections, span_dev, 4 * slots), jnp.float32)
            make = functools.partial(table_kernel, 2 * slots)
            hits, weighs = in_vmem(make, [table] * 2, (routes,), 8)
            positions = by_tick(offsets)[:, None] + member * span_dev
            positions = positions + jnp.arange(span_dev, dtype=jnp.int32)[None, :]
            turns = rotation(kv_width - LAT, positions.reshape(-1))
        arrived = lax.all_to_all(chosen, "z", split_axis=0, concat_axis=0, tiled=True)
        if last_tick:
            late_rows = jnp.pad(late_rows, ((0, 8), (0, 0)))
            arrived = jnp.concatenate([arrived, late_rows], axis=0)
        if tick == 0:
            held = lax.optimization_barrier((arrived, turns, hits, weighs))
            arrived, turns, hits, weighs = held
        copies = in_vmem(
            copies_kernel,
            jax.ShapeDtypeStruct((n_columns * arrived.shape[0], half), jnp.bfloat16),
            (arrived,),
            8,
        )
        token_rows = lax.all_to_all(copies, "y", split_axis=0, concat_axis=0, tiled=True)
        parts = in_vmem(
            lambda *refs: expert_kernel(n_columns, *refs),
            jax.ShapeDtypeStruct((n_columns * slots, model_width), jnp.bfloat16),
            (token_rows, local_gate, local_up, local_down),
            24,
            flops,
        )
        if tick == 1:
            parts, latent_full = lax.optimization_barrier((parts, latent_full))
        if tick == EARLY - 1:
            held = lax.optimization_barrier((parts, tick_rows, gains, latent_full, turns))
            parts, tick_rows, gains, latent_full, turns = held
            early_rows = project(0, EARLY, gains, latent_full, turns)
            parts, early_rows = lax.optimization_barrier((parts, early_rows))
            early = lax.all_gather(early_rows, ("z", "y"), axis=0)
        if last_tick:
            held = (parts, token_rows, owner_map)
            parts, token_rows, owner_map = lax.optimization_barrier(held)
            block_order = by_tick(owner_map[0])
        quarters = lax.all_to_all(parts, "y", split_axis=0, concat_axis=0, tiled=True)
        if last_tick:
            quarters, early = lax.optimization_barrier((quarters, early))
        summed = in_vmem(
            lambda *refs: total_kernel(n_columns, *refs),
            jax.ShapeDtypeStruct((2 * slots, half), jnp.bfloat16),
            (quarters,),
            12,
        )
        if last_tick:
            late_rows = token_rows.reshape(n_columns, -1, half)[:, 2 * slots : 2 * slots + 8]
            late_rows = apart(late_rows, n_sections - EARLY)
            late = pack_late(late_rows, block_order, EARLY, n_sections)
            summed = jnp.concatenate([summed.reshape(n_planes, -1, half), late], axis=1)
            summed = summed.reshape(-1, half)
        returned = lax.all_to_all(summed, "z", split_axis=0, concat_axis=0, tiled=True)
        if last_tick:
            returned = returned.reshape(n_planes, -1, half)
            late = unpack_late(returned[:, -8:], EARLY, n_sections)
            returned = returned[:, :-8].reshape(-1, half)
        layer_out = in_vmem(
            combine_kernel,
            jax.ShapeDtypeStruct((span_dev, model_width), jnp.bfloat16),
            (tokens, returned),
            8,
            tick=tick,
            tables=(weighs,),
        )
        if not last_tick:
            layer_in = shifted(layer_out, "section", 1)
    early = deliver_whole(early, block_order, 0, EARLY)
    delivered = [early, late]
    blank = jnp.zeros((n_spans, span_dev, kv_width), jnp.bfloat16)
    kv_ticks = jnp.concatenate(delivered + [blank], axis=0)
    kv_store = lax.dynamic_slice_in_dim(kv_ticks, section_id, n_spans, 0)
    return (layer_out[None], kv_store[None])


def solution(mesh):
    n_members = mesh.shape["ep"]
    grid = Mesh(
        mesh.devices.reshape(mesh.shape["section"], n_members // EXP_SPLIT, EXP_SPLIT),
        ("section", "z", "y"),
    )
    ep = ("z", "y")
    in_specs = (
        P(None, ep, None),
        P("section", None),
        P("section", None),
        P("section", None),
        P("section", ep, None),
        P("section", None, ep),
        P("section", None, ep),
        P("section", ep, None),
        P("section", None, None, None),
        P("section", None, ep, None),
        P("section", None, None),
        P(),
    )
    out_specs = (P("section", ep, None), P("section", None, ep, None))
    return jax.shard_map(body, mesh=grid, in_specs=in_specs, out_specs=out_specs, check_vma=False)
```

```python
import functools

import jax
import jax.numpy as jnp
import numpy as np
from jax import lax
from jax.experimental import pallas as pl
from jax.experimental.pallas import tpu as pltpu
from jax.sharding import Mesh, PartitionSpec as P

LAT = 512
EXP_SPLIT = 4
TOPK = 2
KVBLK = 4
EARLY = 7


eps = 1e-06


def shifted(block, axis, distance):
    devices = range(lax.axis_size(axis))
    route = [(i - distance, i) for i in devices if i - distance in devices]
    return lax.ppermute(block, axis, route)


def rms_scale(values, gain_vec):
    values = values.astype(jnp.float32)
    return values * lax.rsqrt(jnp.mean(values * values, axis=-1, keepdims=True) + eps) * gain_vec


def rotation(width, positions):
    half_dim = width // 2
    frequency = 10000.0 ** (-jnp.arange(half_dim, dtype=jnp.float32) / half_dim)
    angles = positions.astype(jnp.float32)[:, None] * frequency[None, :]
    return jnp.tile(jnp.cos(angles), (1, 2)), jnp.tile(jnp.sin(angles), (1, 2))


def one_hot(rows, cols, wanted, kept=None):
    row = lax.broadcasted_iota(jnp.int32, (rows, cols), 0)
    col = lax.broadcasted_iota(jnp.int32, (rows, cols), 1)
    hit = col == wanted(row)
    if kept is not None:
        hit = hit & kept(row)
    return jnp.where(hit, 1.0, 0.0).astype(jnp.bfloat16)


def matmul(left, right):
    return jnp.dot(left, right, preferred_element_type=jnp.float32)


def in_vmem(kernel, out_shape, operands, limit_mib, flops=0, tick=None, tables=()):
    moved = sum(x.size * x.dtype.itemsize for x in operands)
    specs = [pl.BlockSpec(memory_space=pltpu.VMEM)] * len(operands)
    for table in tables:
        specs.append(pl.BlockSpec((1,) + table.shape[1:], lambda i: (tick, 0, 0)))
    return pl.pallas_call(
        kernel,
        grid=(1,),
        out_shape=out_shape,
        in_specs=specs,
        out_specs=jax.tree.map(lambda _: pl.BlockSpec(memory_space=pltpu.VMEM), out_shape),
        compiler_params=pltpu.CompilerParams(vmem_limit_bytes=limit_mib * 1024 * 1024),
        cost_estimate=pl.CostEstimate(flops=flops, bytes_accessed=moved, transcendentals=0),
    )(*operands, *tables)


def slot_hits(routes, folded, offset):
    rows = routes.shape[0]
    line = lax.broadcasted_iota(jnp.int32, (rows, folded), 1)
    expert = (line // 8).astype(jnp.float32)
    slot = (line % 8 - offset).astype(jnp.float32)
    picked = jnp.zeros((rows, folded), jnp.float32)
    weight = jnp.zeros((rows, folded), jnp.float32)
    for k in range(TOPK):
        same = routes[:, k : k + 1] == expert
        picked = jnp.where(same, 1.0, picked)
        weight = jnp.where(same, routes[:, TOPK + k : TOPK + k + 1], weight)
    row = lax.broadcasted_iota(jnp.int32, (rows, rows), 0)
    col = lax.broadcasted_iota(jnp.int32, (rows, rows), 1)
    earlier = jnp.where(col < row, 1.0, 0.0)
    rank = matmul(earlier, picked)
    hit = (picked > 0.5) & (rank == slot) & (slot >= 0.0) & (slot < 4.0)
    return jnp.where(hit, 1.0, 0.0), jnp.where(hit, weight, 0.0)


def table_kernel(folded, routes, hits_out, weights_out):
    for tick in range(routes.shape[0]):
        for k, offset in enumerate((0, 4)):
            hits, weights = slot_hits(routes[tick], folded, offset)
            cols = slice(k * folded, (k + 1) * folded)
            hits_out[tick, :, cols] = hits
            weights_out[tick, :, cols] = weights


def choose_kernel(made, tokens, gain, table, out):
    folded, half = out.shape
    normed = rms_scale(tokens[...], gain[...]).astype(jnp.bfloat16).astype(jnp.float32)
    picked = 0.0
    for k, offset in enumerate((0, 4)):
        if made:
            hits = table[0, :, k * folded : (k + 1) * folded]
        else:
            hits, _ = slot_hits(table[0], folded, offset)
        picked = picked + lax.dot_general(
            hits,
            normed[:, k * half : (k + 1) * half],
            (((0,), (0,)), ((), ())),
            preferred_element_type=jnp.float32,
        )
    out[...] = picked.astype(jnp.bfloat16)


def latent_kernel(rows, attn_gain, kv_gain, w_latent, cosine, sine, out):
    normed = rms_scale(rows[...], attn_gain[...]).astype(jnp.bfloat16)
    latent = matmul(normed, w_latent[...])
    out[:, :LAT] = rms_scale(latent[:, :LAT], kv_gain[...]).astype(jnp.bfloat16)
    tail = latent[:, LAT:]
    width = tail.shape[1]
    row = lax.broadcasted_iota(jnp.int32, (width, width), 0)
    col = lax.broadcasted_iota(jnp.int32, (width, width), 1)
    turn = jnp.where(row == col + width // 2, -1.0, jnp.where(row + width // 2 == col, 1.0, 0.0))
    turned = jnp.dot(
        tail, turn, precision=lax.Precision.HIGHEST, preferred_element_type=jnp.float32
    )
    out[:, LAT:] = (tail * cosine[...] + turned * sine[...]).astype(jnp.bfloat16)


def expert_kernel(columns, tokens, w_gate, w_up, w_down, out):
    height, half = tokens.shape
    slots = out.shape[0]
    each, stride = slots // columns, height // columns

    def place(row):
        within = row % each
        return (row // each) * stride + (within // 4) * 8 + within % 4

    first = matmul(one_hot(slots, height, place), tokens[...]).astype(jnp.bfloat16)
    second = matmul(one_hot(slots, height, lambda row: place(row) + 4), tokens[...])
    second = second.astype(jnp.bfloat16)
    gate_proj = matmul(first, w_gate[:half, :]) + matmul(second, w_gate[half:, :])
    up_proj = matmul(first, w_up[:half, :]) + matmul(second, w_up[half:, :])
    hidden = (gate_proj / (1.0 + jnp.exp(-gate_proj)) * up_proj).astype(jnp.bfloat16)
    width = 512
    for start in range(0, 2 * half, width):
        cols = slice(start, start + width)
        out[:, cols] = matmul(hidden, w_down[:, cols]).astype(jnp.bfloat16)


def total_kernel(columns, quarters, *rest):
    out = rest[-1]
    height, half = out.shape
    slots = quarters.shape[0] // columns
    group = height // (slots // 4)
    total = quarters[:slots, :].astype(jnp.float32)
    for k in range(1, columns):
        total = total + quarters[k * slots : (k + 1) * slots, :].astype(jnp.float32)
    total = total.astype(jnp.bfloat16)
    place = lambda row: (row // group) * 4 + row % 4
    first = one_hot(height, slots, place, lambda row: row % group < 4)
    second = one_hot(height, slots, place, lambda row: (row % group >= 4) & (row % group < 8))
    spread = matmul(first, total[:, :half]) + matmul(second, total[:, half:])
    if len(rest) > 1:
        gathered, pick = rest[0], rest[1]
        stride = gathered.shape[0] // columns
        source = lambda row: (row // 8) * stride + stride - 8 + row % 8
        kv_rows = matmul(one_hot(8 * columns, gathered.shape[0], source), gathered[...])
        picked = matmul(pick[...], kv_rows.astype(jnp.bfloat16)).astype(jnp.bfloat16)
        place = lambda row: (row // group) * 8 + row % 8
        third = one_hot(height, picked.shape[0], place, lambda row: row % group >= 8)
        spread = spread + matmul(third, picked)
    out[...] = spread.astype(jnp.bfloat16)


def combine_kernel(tokens, returned, table, out):
    folded, half = returned.shape
    span_dev = tokens.shape[0]
    for k in range(2):
        cols = slice(k * half, (k + 1) * half)
        rest = table[0, :, k * folded : (k + 1) * folded]
        terms = []
        for _ in range(3):
            term = rest.astype(jnp.bfloat16)
            rest = rest - term.astype(jnp.float32)
            terms.append(term.astype(jnp.float32))
        terms = jnp.concatenate(terms, axis=0).astype(jnp.bfloat16)
        sums = matmul(terms, returned[...])
        moe_sum = sums[:span_dev] + sums[span_dev : 2 * span_dev] + sums[2 * span_dev :]
        out[:, cols] = (tokens[:, cols].astype(jnp.float32) + moe_sum).astype(jnp.bfloat16)


def body(
    spans,
    attn_gain,
    kv_gain,
    moe_gain,
    w_latent,
    w_gate,
    w_up,
    w_down,
    expert_ids,
    gate_vals,
    owner_map,
    offsets,
):
    section_id = lax.axis_index("section")
    plane = lax.axis_index("z")
    column = lax.axis_index("y")
    n_planes = lax.axis_size("z")
    n_columns = lax.axis_size("y")
    member = plane * n_columns + column
    n_members = n_planes * n_columns
    n_sections = lax.axis_size("section")
    n_spans, span_dev, model_width = spans.shape
    kv_width = w_latent.shape[2]
    experts = n_members // EXP_SPLIT
    capacity = min(span_dev, 2 * span_dev * TOPK // experts)
    per_owner = span_dev // KVBLK
    local_gate = w_gate[0]
    local_up = w_up[0]
    local_down = w_down[0]
    latent_full = lax.all_gather(w_latent[0], ("z", "y"), axis=0, tiled=True)

    def by_tick(values):
        padded = jnp.concatenate([jnp.zeros_like(values), values], axis=0)
        return lax.dynamic_slice_in_dim(padded, n_spans - section_id, n_sections, 0)

    own_ids = by_tick(lax.dynamic_slice_in_dim(expert_ids[0], member * span_dev, span_dev, 1))
    routes = jnp.concatenate([own_ids.astype(jnp.float32), by_tick(gate_vals[0])], axis=2)

    def project(first, last, gains, weights, turns):
        rows = jnp.concatenate(tick_rows[first:last], axis=0)
        part = slice(first * span_dev, last * span_dev)
        return in_vmem(
            latent_kernel,
            jax.ShapeDtypeStruct((rows.shape[0], kv_width), jnp.bfloat16),
            (rows, *gains, weights, turns[0][part], turns[1][part]),
            16,
        )

    def owned_rows(order):
        block = jnp.repeat(order, KVBLK, axis=-1)
        return block * KVBLK + np.arange(block.shape[-1], dtype=np.int32) % KVBLK

    def early_picks(block_order, count):
        order = lax.dynamic_slice_in_dim(
            block_order[:count], member * per_owner, per_owner, 1
        )
        every = np.arange(n_members * span_dev, dtype=np.int32)
        pick = (owned_rows(order)[..., None] == every).astype(jnp.bfloat16)
        return pick.reshape(count, span_dev, n_members, span_dev)

    def deliver_early(gathered, pick):
        gathered = gathered.reshape(n_members, pick.shape[0], span_dev, kv_width)
        return jnp.einsum(
            "tdmr,mtrk->tdk", pick, gathered, preferred_element_type=jnp.float32
        ).astype(jnp.bfloat16)

    def late_picks(block_order):
        order = block_order[-1].reshape(n_planes, n_columns, per_owner)
        order = lax.dynamic_index_in_dim(order, column, 1, keepdims=False)
        held = plane * n_columns * span_dev + np.arange(n_columns * span_dev, dtype=np.int32)
        pick = (owned_rows(order)[..., None] == held).astype(jnp.bfloat16)
        return pick.reshape(n_planes * span_dev, n_columns * span_dev)

    half = model_width // 2
    slots = experts * capacity
    tick_rows = []
    gains = (attn_gain, kv_gain)
    flops = 2 * 3 * n_columns * slots * model_width * local_gate.shape[1]
    for tick in range(n_sections):
        last_tick = tick + 1 == n_sections
        tokens = jnp.where(is_first, spans[tick], layer_in) if tick else spans[0]
        tick_rows.append(tokens)
        if last_tick:
            late_rows = project(EARLY, n_sections, gains, latent_full, turns)
            late_rows = jnp.pad(late_rows, ((0, 0), (0, half - kv_width)))
            tokens, late_rows = lax.optimization_barrier((tokens, late_rows))
        chosen = in_vmem(
            functools.partial(choose_kernel, tick > 0),
            jax.ShapeDtypeStruct((2 * slots, half), jnp.bfloat16),
            (tokens, moe_gain),
            8,
            tick=tick,
            tables=(hits if tick else routes,),
        )
        if tick == 0:
            held = (chosen, offsets, routes, owner_map, section_id == 0)
            held = lax.optimization_barrier(held)
            chosen, offsets, routes, owner_map, is_first = held
            block_order = by_tick(owner_map[0])
            picks = early_picks(block_order, EARLY), late_picks(block_order)
            table = jax.ShapeDtypeStruct((n_sections, span_dev, 4 * slots), jnp.float32)
            make = functools.partial(table_kernel, 2 * slots)
            hits, weighs = in_vmem(make, [table] * 2, (routes,), 8)
            positions = by_tick(offsets)[:, None] + member * span_dev
            positions = positions + jnp.arange(span_dev, dtype=jnp.int32)[None, :]
            turns = rotation(kv_width - LAT, positions.reshape(-1))
        arrived = lax.all_to_all(chosen, "z", split_axis=0, concat_axis=0, tiled=True)
        if last_tick:
            arrived = jnp.concatenate([arrived, late_rows], axis=0)
        if tick == 0:
            held = lax.optimization_barrier((arrived, turns, hits, weighs, picks))
            arrived, turns, hits, weighs, picks = held
        token_rows = lax.all_gather(arrived, "y", axis=0, tiled=True)
        parts = in_vmem(
            lambda *refs: expert_kernel(n_columns, *refs),
            jax.ShapeDtypeStruct((n_columns * slots, model_width), jnp.bfloat16),
            (token_rows, local_gate, local_up, local_down),
            24,
            flops,
        )
        if tick == 1:
            parts, latent_full = lax.optimization_barrier((parts, latent_full))
        if tick == EARLY - 1:
            held = lax.optimization_barrier((parts, tick_rows, gains, latent_full, turns))
            parts, tick_rows, gains, latent_full, turns = held
            early_rows = project(0, EARLY, gains, latent_full, turns)
            parts, early_rows = lax.optimization_barrier((parts, early_rows))
            early = lax.all_gather(early_rows, ("z", "y"), axis=0)
        quarters = lax.all_to_all(parts, "y", split_axis=0, concat_axis=0, tiled=True)
        if last_tick:
            quarters, early = lax.optimization_barrier((quarters, early))
        summed = in_vmem(
            functools.partial(total_kernel, n_columns),
            jax.ShapeDtypeStruct(((4 if last_tick else 2) * slots, half), jnp.bfloat16),
            (quarters, token_rows, picks[1]) if last_tick else (quarters,),
            12,
        )
        returned = lax.all_to_all(summed, "z", split_axis=0, concat_axis=0, tiled=True)
        if last_tick:
            returned = returned.reshape(n_planes, -1, half)
            late = jnp.sum(returned[:, -8:, :kv_width].astype(jnp.float32), axis=0)
            late = late.astype(jnp.bfloat16)[None]
            returned = returned[:, :-8].reshape(-1, half)
        layer_out = in_vmem(
            combine_kernel,
            jax.ShapeDtypeStruct((span_dev, model_width), jnp.bfloat16),
            (tokens, returned),
            8,
            tick=tick,
            tables=(weighs,),
        )
        if not last_tick:
            layer_in = shifted(layer_out, "section", 1)
    early = deliver_early(early, picks[0])
    delivered = [early, late]
    blank = jnp.zeros((n_spans, span_dev, kv_width), jnp.bfloat16)
    kv_ticks = jnp.concatenate(delivered + [blank], axis=0)
    kv_store = lax.dynamic_slice_in_dim(kv_ticks, section_id, n_spans, 0)
    return (layer_out[None], kv_store[None])


def solution(mesh):
    n_members = mesh.shape["ep"]
    grid = Mesh(
        mesh.devices.reshape(mesh.shape["section"], n_members // EXP_SPLIT, EXP_SPLIT),
        ("section", "z", "y"),
    )
    ep = ("z", "y")
    in_specs = (
        P(None, ep, None),
        P("section", None),
        P("section", None),
        P("section", None),
        P("section", ep, None),
        P("section", None, ep),
        P("section", None, ep),
        P("section", ep, None),
        P("section", None, None, None),
        P("section", None, ep, None),
        P("section", None, None),
        P(),
    )
    out_specs = (P("section", ep, None), P("section", None, ep, None))
    return jax.shard_map(body, mesh=grid, in_specs=in_specs, out_specs=out_specs, check_vma=False)
```

```python
import functools

import jax
import jax.numpy as jnp
import numpy as np
from jax import lax
from jax.experimental import pallas as pl
from jax.experimental.pallas import tpu as pltpu
from jax.sharding import Mesh, PartitionSpec as P

LAT = 512
EXP_SPLIT = 4
TOPK = 2
KVBLK = 4
EARLY = 7


eps = 1e-06


def shifted(block, axis, distance):
    devices = range(lax.axis_size(axis))
    route = [(i - distance, i) for i in devices if i - distance in devices]
    return lax.ppermute(block, axis, route)


def rms_scale(values, gain_vec):
    values = values.astype(jnp.float32)
    return values * lax.rsqrt(jnp.mean(values * values, axis=-1, keepdims=True) + eps) * gain_vec


def rotation(width, positions):
    half_dim = width // 2
    step = jnp.arange(width, dtype=jnp.float32) % half_dim
    frequency = 10000.0 ** (-step / half_dim)
    angles = positions.astype(jnp.float32)[:, None] * frequency[None, :]
    return jnp.cos(angles), jnp.sin(angles)


def one_hot(rows, cols, wanted, kept=None):
    row = lax.broadcasted_iota(jnp.int32, (rows, cols), 0)
    col = lax.broadcasted_iota(jnp.int32, (rows, cols), 1)
    hit = col == wanted(row)
    if kept is not None:
        hit = hit & kept(row)
    return jnp.where(hit, 1.0, 0.0).astype(jnp.bfloat16)


def matmul(left, right):
    return jnp.dot(left, right, preferred_element_type=jnp.float32)


def in_vmem(kernel, out_shape, operands, limit_mib, flops=0, tick=None, tables=()):
    moved = sum(x.size * x.dtype.itemsize for x in operands)
    specs = [pl.BlockSpec(memory_space=pltpu.VMEM)] * len(operands)
    for table in tables:
        specs.append(pl.BlockSpec((1,) + table.shape[1:], lambda i: (tick, 0, 0)))
    return pl.pallas_call(
        kernel,
        grid=(1,),
        out_shape=out_shape,
        in_specs=specs,
        out_specs=jax.tree.map(lambda _: pl.BlockSpec(memory_space=pltpu.VMEM), out_shape),
        compiler_params=pltpu.CompilerParams(vmem_limit_bytes=limit_mib * 1024 * 1024),
        cost_estimate=pl.CostEstimate(flops=flops, bytes_accessed=moved, transcendentals=0),
    )(*operands, *tables)


def slot_hits(routes, folded, offset):
    rows = routes.shape[0]
    line = lax.broadcasted_iota(jnp.int32, (rows, folded), 1)
    expert = (line // 8).astype(jnp.float32)
    slot = (line % 8 - offset).astype(jnp.float32)
    picked = jnp.zeros((rows, folded), jnp.float32)
    weight = jnp.zeros((rows, folded), jnp.float32)
    for k in range(TOPK):
        same = routes[:, k : k + 1] == expert
        picked = jnp.where(same, 1.0, picked)
        weight = jnp.where(same, routes[:, TOPK + k : TOPK + k + 1], weight)
    row = lax.broadcasted_iota(jnp.int32, (rows, rows), 0)
    col = lax.broadcasted_iota(jnp.int32, (rows, rows), 1)
    earlier = jnp.where(col < row, 1.0, 0.0)
    rank = matmul(earlier, picked)
    hit = (picked > 0.5) & (rank == slot) & (slot >= 0.0) & (slot < 4.0)
    return jnp.where(hit, 1.0, 0.0), jnp.where(hit, weight, 0.0)


def table_kernel(folded, routes, hits_out, weights_out):
    for tick in range(routes.shape[0]):
        for k, offset in enumerate((0, 4)):
            hits, weights = slot_hits(routes[tick], folded, offset)
            cols = slice(k * folded, (k + 1) * folded)
            hits_out[tick, :, cols] = hits
            weights_out[tick, :, cols] = weights


def choose_kernel(made, tokens, gain, table, out):
    folded, half = out.shape
    normed = rms_scale(tokens[...], gain[...]).astype(jnp.bfloat16).astype(jnp.float32)
    picked = 0.0
    for k, offset in enumerate((0, 4)):
        if made:
            hits = table[0, :, k * folded : (k + 1) * folded]
        else:
            hits, _ = slot_hits(table[0], folded, offset)
        picked = picked + lax.dot_general(
            hits,
            normed[:, k * half : (k + 1) * half],
            (((0,), (0,)), ((), ())),
            preferred_element_type=jnp.float32,
        )
    out[...] = picked.astype(jnp.bfloat16)


def latent_kernel(rows, attn_gain, kv_gain, w_latent, cosine, sine, out):
    normed = rms_scale(rows[...], attn_gain[...]).astype(jnp.bfloat16)
    latent = matmul(normed, w_latent[...])
    out[:, :LAT] = rms_scale(latent[:, :LAT], kv_gain[...]).astype(jnp.bfloat16)
    tail = latent[:, LAT:]
    width = tail.shape[1]
    row = lax.broadcasted_iota(jnp.int32, (width, width), 0)
    col = lax.broadcasted_iota(jnp.int32, (width, width), 1)
    turn = jnp.where(row == col + width // 2, -1.0, jnp.where(row + width // 2 == col, 1.0, 0.0))
    turned = jnp.dot(
        tail, turn, precision=lax.Precision.HIGHEST, preferred_element_type=jnp.float32
    )
    out[:, LAT:] = (tail * cosine[...] + turned * sine[...]).astype(jnp.bfloat16)


def expert_kernel(columns, tokens, w_gate, w_up, w_down, out):
    height, half = tokens.shape
    slots = out.shape[0]
    each, stride = slots // columns, height // columns

    def place(row):
        within = row % each
        return (row // each) * stride + (within // 4) * 8 + within % 4

    first = matmul(one_hot(slots, height, place), tokens[...]).astype(jnp.bfloat16)
    second = matmul(one_hot(slots, height, lambda row: place(row) + 4), tokens[...])
    second = second.astype(jnp.bfloat16)
    gate_proj = matmul(first, w_gate[:half, :]) + matmul(second, w_gate[half:, :])
    up_proj = matmul(first, w_up[:half, :]) + matmul(second, w_up[half:, :])
    hidden = (gate_proj / (1.0 + jnp.exp(-gate_proj)) * up_proj).astype(jnp.bfloat16)
    width = 512
    for start in range(0, 2 * half, width):
        cols = slice(start, start + width)
        out[:, cols] = matmul(hidden, w_down[:, cols]).astype(jnp.bfloat16)


def total_kernel(columns, quarters, *rest):
    out = rest[-1]
    height, half = out.shape
    slots = quarters.shape[0] // columns
    group = height // (slots // 4)
    total = quarters[:slots, :].astype(jnp.float32)
    for k in range(1, columns):
        total = total + quarters[k * slots : (k + 1) * slots, :].astype(jnp.float32)
    total = total.astype(jnp.bfloat16)
    place = lambda row: (row // group) * 4 + row % 4
    first = one_hot(height, slots, place, lambda row: row % group < 4)
    second = one_hot(height, slots, place, lambda row: (row % group >= 4) & (row % group < 8))
    spread = matmul(first, total[:, :half]) + matmul(second, total[:, half:])
    if len(rest) > 1:
        gathered, pick = rest[0], rest[1]
        stride = gathered.shape[0] // columns
        source = lambda row: (row // 8) * stride + stride - 8 + row % 8
        kv_rows = matmul(one_hot(8 * columns, gathered.shape[0], source), gathered[...])
        picked = matmul(pick[...], kv_rows.astype(jnp.bfloat16)).astype(jnp.bfloat16)
        place = lambda row: (row // group) * 8 + row % 8
        third = one_hot(height, picked.shape[0], place, lambda row: row % group >= 8)
        spread = spread + matmul(third, picked)
    out[...] = spread.astype(jnp.bfloat16)


def combine_kernel(tokens, returned, table, out):
    folded, half = returned.shape
    span_dev = tokens.shape[0]
    for k in range(2):
        cols = slice(k * half, (k + 1) * half)
        rest = table[0, :, k * folded : (k + 1) * folded]
        terms = []
        for _ in range(3):
            term = rest.astype(jnp.bfloat16)
            rest = rest - term.astype(jnp.float32)
            terms.append(term.astype(jnp.float32))
        terms = jnp.concatenate(terms, axis=0).astype(jnp.bfloat16)
        sums = matmul(terms, returned[...])
        moe_sum = sums[:span_dev] + sums[span_dev : 2 * span_dev] + sums[2 * span_dev :]
        out[:, cols] = (tokens[:, cols].astype(jnp.float32) + moe_sum).astype(jnp.bfloat16)


def body(
    spans,
    attn_gain,
    kv_gain,
    moe_gain,
    w_latent,
    w_gate,
    w_up,
    w_down,
    expert_ids,
    gate_vals,
    owner_map,
    offsets,
):
    section_id = lax.axis_index("section")
    plane = lax.axis_index("z")
    column = lax.axis_index("y")
    n_planes = lax.axis_size("z")
    n_columns = lax.axis_size("y")
    member = plane * n_columns + column
    n_members = n_planes * n_columns
    n_sections = lax.axis_size("section")
    n_spans, span_dev, model_width = spans.shape
    kv_width = w_latent.shape[2]
    experts = n_members // EXP_SPLIT
    capacity = min(span_dev, 2 * span_dev * TOPK // experts)
    per_owner = span_dev // KVBLK
    local_gate = w_gate[0]
    local_up = w_up[0]
    local_down = w_down[0]
    latent_full = lax.all_gather(w_latent[0], ("z", "y"), axis=0, tiled=True)

    def by_tick(values):
        padded = jnp.concatenate([jnp.zeros_like(values), values], axis=0)
        return lax.dynamic_slice_in_dim(padded, n_spans - section_id, n_sections, 0)

    own_ids = by_tick(lax.dynamic_slice_in_dim(expert_ids[0], member * span_dev, span_dev, 1))
    routes = jnp.concatenate([own_ids.astype(jnp.float32), by_tick(gate_vals[0])], axis=2)

    def project(first, last, gains, weights, turns):
        rows = jnp.concatenate(tick_rows[first:last], axis=0)
        part = slice(first * span_dev, last * span_dev)
        return in_vmem(
            latent_kernel,
            jax.ShapeDtypeStruct((rows.shape[0], kv_width), jnp.bfloat16),
            (rows, *gains, weights, turns[0][part], turns[1][part]),
            16,
        )

    def owned_rows(order):
        block = jnp.repeat(order, KVBLK, axis=-1)
        return block * KVBLK + np.arange(block.shape[-1], dtype=np.int32) % KVBLK

    def early_picks(block_order, count):
        order = lax.dynamic_slice_in_dim(
            block_order[:count], member * per_owner, per_owner, 1
        )
        every = np.arange(n_members * span_dev, dtype=np.int32)
        pick = (owned_rows(order)[..., None] == every).astype(jnp.bfloat16)
        return pick.reshape(count, span_dev, n_members, span_dev)

    def deliver_early(gathered, pick):
        gathered = gathered.reshape(n_members, pick.shape[0], span_dev, kv_width)
        return jnp.einsum(
            "tdmr,mtrk->tdk", pick, gathered, preferred_element_type=jnp.float32
        ).astype(jnp.bfloat16)

    def late_picks(block_order):
        order = block_order[-1].reshape(n_planes, n_columns, per_owner)
        order = lax.dynamic_index_in_dim(order, column, 1, keepdims=False)
        held = plane * n_columns * span_dev + np.arange(n_columns * span_dev, dtype=np.int32)
        pick = (owned_rows(order)[..., None] == held).astype(jnp.bfloat16)
        return pick.reshape(n_planes * span_dev, n_columns * span_dev)

    half = model_width // 2
    slots = experts * capacity
    tick_rows = []
    gains = (attn_gain, kv_gain)
    flops = 2 * 3 * n_columns * slots * model_width * local_gate.shape[1]
    for tick in range(n_sections):
        last_tick = tick + 1 == n_sections
        tokens = jnp.where(is_first, spans[tick], layer_in) if tick else spans[0]
        tick_rows.append(tokens)
        if last_tick:
            late_rows = project(EARLY, n_sections, gains, latent_full, turns)
            late_rows = jnp.pad(late_rows, ((0, 0), (0, half - kv_width)))
            tokens, late_rows = lax.optimization_barrier((tokens, late_rows))
        chosen = in_vmem(
            functools.partial(choose_kernel, tick > 0),
            jax.ShapeDtypeStruct((2 * slots, half), jnp.bfloat16),
            (tokens, moe_gain),
            8,
            tick=tick,
            tables=(hits if tick else routes,),
        )
        if tick == 0:
            held = (chosen, offsets, routes, owner_map, section_id == 0)
            held = lax.optimization_barrier(held)
            chosen, offsets, routes, owner_map, is_first = held
            block_order = by_tick(owner_map[0])
            picks = early_picks(block_order, EARLY), late_picks(block_order)
            table = jax.ShapeDtypeStruct((n_sections, span_dev, 4 * slots), jnp.float32)
            make = functools.partial(table_kernel, 2 * slots)
            hits, weighs = in_vmem(make, [table] * 2, (routes,), 8)
            positions = by_tick(offsets)[:, None] + member * span_dev
            positions = positions + jnp.arange(span_dev, dtype=jnp.int32)[None, :]
            turns = rotation(kv_width - LAT, positions.reshape(-1))
        arrived = lax.all_to_all(chosen, "z", split_axis=0, concat_axis=0, tiled=True)
        if last_tick:
            arrived = jnp.concatenate([arrived, late_rows], axis=0)
        if tick == 0:
            held = lax.optimization_barrier((arrived, turns, hits, weighs, picks))
            arrived, turns, hits, weighs, picks = held
        token_rows = lax.all_gather(arrived, "y", axis=0, tiled=True)
        parts = in_vmem(
            lambda *refs: expert_kernel(n_columns, *refs),
            jax.ShapeDtypeStruct((n_columns * slots, model_width), jnp.bfloat16),
            (token_rows, local_gate, local_up, local_down),
            24,
            flops,
        )
        if tick == 1:
            parts, latent_full = lax.optimization_barrier((parts, latent_full))
        if tick == EARLY - 1:
            held = lax.optimization_barrier((parts, tick_rows, gains, latent_full, turns))
            parts, tick_rows, gains, latent_full, turns = held
            early_rows = project(0, EARLY, gains, latent_full, turns)
            parts, early_rows = lax.optimization_barrier((parts, early_rows))
            early = lax.all_gather(early_rows, ("z", "y"), axis=0)
        quarters = lax.all_to_all(parts, "y", split_axis=0, concat_axis=0, tiled=True)
        if last_tick:
            quarters, early = lax.optimization_barrier((quarters, early))
        summed = in_vmem(
            functools.partial(total_kernel, n_columns),
            jax.ShapeDtypeStruct(((4 if last_tick else 2) * slots, half), jnp.bfloat16),
            (quarters, token_rows, picks[1]) if last_tick else (quarters,),
            12,
        )
        returned = lax.all_to_all(summed, "z", split_axis=0, concat_axis=0, tiled=True)
        if last_tick:
            returned = returned.reshape(n_planes, -1, half)
            late = jnp.sum(returned[:, -8:, :kv_width].astype(jnp.float32), axis=0)
            late = late.astype(jnp.bfloat16)[None]
            returned = returned[:, :-8].reshape(-1, half)
        layer_out = in_vmem(
            combine_kernel,
            jax.ShapeDtypeStruct((span_dev, model_width), jnp.bfloat16),
            (tokens, returned),
            8,
            tick=tick,
            tables=(weighs,),
        )
        if not last_tick:
            layer_in = shifted(layer_out, "section", 1)
    early = deliver_early(early, picks[0])
    delivered = [early, late]
    blank = jnp.zeros((n_spans, span_dev, kv_width), jnp.bfloat16)
    kv_ticks = jnp.concatenate(delivered + [blank], axis=0)
    kv_store = lax.dynamic_slice_in_dim(kv_ticks, section_id, n_spans, 0)
    return (layer_out[None], kv_store[None])


def solution(mesh):
    n_members = mesh.shape["ep"]
    grid = Mesh(
        mesh.devices.reshape(mesh.shape["section"], n_members // EXP_SPLIT, EXP_SPLIT),
        ("section", "z", "y"),
    )
    ep = ("z", "y")
    in_specs = (
        P(None, ep, None),
        P("section", None),
        P("section", None),
        P("section", None),
        P("section", ep, None),
        P("section", None, ep),
        P("section", None, ep),
        P("section", ep, None),
        P("section", None, None, None),
        P("section", None, ep, None),
        P("section", None, None),
        P(),
    )
    out_specs = (P("section", ep, None), P("section", None, ep, None))
    return jax.shard_map(body, mesh=grid, in_specs=in_specs, out_specs=out_specs, check_vma=False)
```

```python
import functools

import jax
import jax.numpy as jnp
import numpy as np
from jax import lax
from jax.experimental import pallas as pl
from jax.experimental.pallas import tpu as pltpu
from jax.sharding import Mesh, PartitionSpec as P

LAT = 512
EXP_SPLIT = 4
TOPK = 2
KVBLK = 4
EARLY = 7


eps = 1e-06


def shifted(block, axis, distance):
    devices = range(lax.axis_size(axis))
    route = [(i - distance, i) for i in devices if i - distance in devices]
    return lax.ppermute(block, axis, route)


def rms_scale(values, gain_vec):
    values = values.astype(jnp.float32)
    return values * lax.rsqrt(jnp.mean(values * values, axis=-1, keepdims=True) + eps) * gain_vec


def rotation(width, positions):
    half_dim = width // 2
    step = jnp.arange(width, dtype=jnp.float32) % half_dim
    frequency = 10000.0 ** (-step / half_dim)
    angles = positions.astype(jnp.float32)[:, None] * frequency[None, :]
    return jnp.cos(angles), jnp.sin(angles)


def one_hot(rows, cols, wanted, kept=None):
    row = lax.broadcasted_iota(jnp.int32, (rows, cols), 0)
    col = lax.broadcasted_iota(jnp.int32, (rows, cols), 1)
    hit = col == wanted(row)
    if kept is not None:
        hit = hit & kept(row)
    return jnp.where(hit, 1.0, 0.0).astype(jnp.bfloat16)


def matmul(left, right):
    return jnp.dot(left, right, preferred_element_type=jnp.float32)


def in_vmem(kernel, out_shape, operands, limit_mib, flops=0, tick=None, tables=()):
    moved = sum(x.size * x.dtype.itemsize for x in operands)
    specs = [pl.BlockSpec(memory_space=pltpu.VMEM)] * len(operands)
    for table in tables:
        specs.append(pl.BlockSpec((1,) + table.shape[1:], lambda i: (tick, 0, 0)))
    return pl.pallas_call(
        kernel,
        grid=(1,),
        out_shape=out_shape,
        in_specs=specs,
        out_specs=jax.tree.map(lambda _: pl.BlockSpec(memory_space=pltpu.VMEM), out_shape),
        compiler_params=pltpu.CompilerParams(vmem_limit_bytes=limit_mib * 1024 * 1024),
        cost_estimate=pl.CostEstimate(flops=flops, bytes_accessed=moved, transcendentals=0),
    )(*operands, *tables)


def slot_hits(routes, folded, offset):
    rows = routes.shape[0]
    line = lax.broadcasted_iota(jnp.int32, (rows, folded), 1)
    expert = (line // 8).astype(jnp.float32)
    slot = (line % 8 - offset).astype(jnp.float32)
    picked = jnp.zeros((rows, folded), jnp.float32)
    weight = jnp.zeros((rows, folded), jnp.float32)
    for k in range(TOPK):
        same = routes[:, k : k + 1] == expert
        picked = jnp.where(same, 1.0, picked)
        last = routes.shape[1] - TOPK + k
        weight = jnp.where(same, routes[:, last : last + 1], weight)
    row = lax.broadcasted_iota(jnp.int32, (rows, rows), 0)
    col = lax.broadcasted_iota(jnp.int32, (rows, rows), 1)
    earlier = jnp.where(col < row, 1.0, 0.0)
    rank = matmul(earlier, picked)
    hit = (picked > 0.5) & (rank == slot) & (slot >= 0.0) & (slot < 4.0)
    return jnp.where(hit, 1.0, 0.0), jnp.where(hit, weight, 0.0)


def table_kernel(folded, routes, hits_out, weights_out):
    for tick in range(routes.shape[0]):
        for k, offset in enumerate((0, 4)):
            hits, weights = slot_hits(routes[tick], folded, offset)
            cols = slice(k * folded, (k + 1) * folded)
            hits_out[tick, :, cols] = hits
            weights_out[tick, :, cols] = weights


def first_choose_kernel(gain, tokens, ids, out):
    choose_rows(tokens[0], gain, ids, out, False)


def choose_kernel(tokens, gain, table, out):
    choose_rows(tokens[...], gain, table, out, True)


def choose_rows(tokens, gain, table, out, made):
    folded, half = out.shape
    normed = rms_scale(tokens, gain[...]).astype(jnp.bfloat16).astype(jnp.float32)
    picked = 0.0
    for k, offset in enumerate((0, 4)):
        if made:
            hits = table[0, :, k * folded : (k + 1) * folded]
        else:
            hits, _ = slot_hits(table[0], folded, offset)
        picked = picked + lax.dot_general(
            hits,
            normed[:, k * half : (k + 1) * half],
            (((0,), (0,)), ((), ())),
            preferred_element_type=jnp.float32,
        )
    out[...] = picked.astype(jnp.bfloat16)


def latent_kernel(rows, attn_gain, kv_gain, w_latent, cosine, sine, out):
    normed = rms_scale(rows[...], attn_gain[...]).astype(jnp.bfloat16)
    latent = matmul(normed, w_latent[...])
    out[:, :LAT] = rms_scale(latent[:, :LAT], kv_gain[...]).astype(jnp.bfloat16)
    tail = latent[:, LAT:]
    width = tail.shape[1]
    row = lax.broadcasted_iota(jnp.int32, (width, width), 0)
    col = lax.broadcasted_iota(jnp.int32, (width, width), 1)
    turn = jnp.where(row == col + width // 2, -1.0, jnp.where(row + width // 2 == col, 1.0, 0.0))
    turned = jnp.dot(
        tail, turn, precision=lax.Precision.HIGHEST, preferred_element_type=jnp.float32
    )
    out[:, LAT:] = (tail * cosine[...] + turned * sine[...]).astype(jnp.bfloat16)


def expert_kernel(columns, tokens, w_gate, w_up, w_down, out):
    height, half = tokens.shape
    slots = out.shape[0]
    each, stride = slots // columns, height // columns

    def place(row):
        within = row % each
        return (row // each) * stride + (within // 4) * 8 + within % 4

    first = matmul(one_hot(slots, height, place), tokens[...]).astype(jnp.bfloat16)
    second = matmul(one_hot(slots, height, lambda row: place(row) + 4), tokens[...])
    second = second.astype(jnp.bfloat16)
    gate_proj = matmul(first, w_gate[:half, :]) + matmul(second, w_gate[half:, :])
    up_proj = matmul(first, w_up[:half, :]) + matmul(second, w_up[half:, :])
    hidden = (gate_proj / (1.0 + jnp.exp(-gate_proj)) * up_proj).astype(jnp.bfloat16)
    width = 512
    for start in range(0, 2 * half, width):
        cols = slice(start, start + width)
        out[:, cols] = matmul(hidden, w_down[:, cols]).astype(jnp.bfloat16)


def total_kernel(columns, quarters, *rest):
    out = rest[-1]
    height, half = out.shape
    slots = quarters.shape[0] // columns
    group = height // (slots // 4)
    total = quarters[:slots, :].astype(jnp.float32)
    for k in range(1, columns):
        total = total + quarters[k * slots : (k + 1) * slots, :].astype(jnp.float32)
    total = total.astype(jnp.bfloat16)
    place = lambda row: (row // group) * 4 + row % 4
    first = one_hot(height, slots, place, lambda row: row % group < 4)
    second = one_hot(height, slots, place, lambda row: (row % group >= 4) & (row % group < 8))
    spread = matmul(first, total[:, :half]) + matmul(second, total[:, half:])
    if len(rest) > 1:
        gathered, pick = rest[0], rest[1]
        stride = gathered.shape[0] // columns
        source = lambda row: (row // 8) * stride + stride - 8 + row % 8
        width = 640
        kv_rows = matmul(one_hot(8 * columns, gathered.shape[0], source), gathered[:, :width])
        picked = matmul(pick[...], kv_rows.astype(jnp.bfloat16)).astype(jnp.bfloat16)
        place = lambda row: (row // group) * 8 + row % 8
        third = one_hot(height, picked.shape[0], place, lambda row: row % group >= 8)
        kv_part = spread[:, :width] + matmul(third, picked)
        spread = jnp.concatenate([kv_part, spread[:, width:]], axis=1)
    out[...] = spread.astype(jnp.bfloat16)


def combine_kernel(tokens, returned, table, out):
    folded, half = returned.shape
    span_dev = tokens.shape[0]
    for k in range(2):
        cols = slice(k * half, (k + 1) * half)
        rest = table[0, :, k * folded : (k + 1) * folded]
        terms = []
        for _ in range(3):
            term = rest.astype(jnp.bfloat16)
            rest = rest - term.astype(jnp.float32)
            terms.append(term.astype(jnp.float32))
        terms = jnp.concatenate(terms, axis=0).astype(jnp.bfloat16)
        sums = matmul(terms, returned[...])
        moe_sum = sums[:span_dev] + sums[span_dev : 2 * span_dev] + sums[2 * span_dev :]
        out[:, cols] = (tokens[:, cols].astype(jnp.float32) + moe_sum).astype(jnp.bfloat16)


def body(
    spans,
    attn_gain,
    kv_gain,
    moe_gain,
    w_latent,
    w_gate,
    w_up,
    w_down,
    expert_ids,
    gate_vals,
    owner_map,
    offsets,
):
    section_id = lax.axis_index("section")
    plane = lax.axis_index("z")
    column = lax.axis_index("y")
    n_planes = lax.axis_size("z")
    n_columns = lax.axis_size("y")
    member = plane * n_columns + column
    n_members = n_planes * n_columns
    n_sections = lax.axis_size("section")
    n_spans, span_dev, model_width = spans.shape
    kv_width = w_latent.shape[2]
    experts = n_members // EXP_SPLIT
    capacity = min(span_dev, 2 * span_dev * TOPK // experts)
    per_owner = span_dev // KVBLK
    local_gate = w_gate[0]
    local_up = w_up[0]
    local_down = w_down[0]
    latent_full = lax.all_gather(w_latent[0], ("z", "y"), axis=0, tiled=True)

    def by_tick(values):
        padded = jnp.concatenate([jnp.zeros_like(values), values], axis=0)
        return lax.dynamic_slice_in_dim(padded, n_spans - section_id, n_sections, 0)

    own_ids = by_tick(lax.dynamic_slice_in_dim(expert_ids[0], member * span_dev, span_dev, 1))
    own_ids = own_ids.astype(jnp.float32)

    def project(first, last, gains, weights, turns):
        rows = jnp.concatenate(tick_rows[first:last], axis=0)
        part = slice(first * span_dev, last * span_dev)
        return in_vmem(
            latent_kernel,
            jax.ShapeDtypeStruct((rows.shape[0], kv_width), jnp.bfloat16),
            (rows, *gains, weights, turns[0][part], turns[1][part]),
            16,
        )

    def owned_rows(order):
        block = jnp.repeat(order, KVBLK, axis=-1)
        return block * KVBLK + np.arange(block.shape[-1], dtype=np.int32) % KVBLK

    def early_picks(block_order, count):
        order = lax.dynamic_slice_in_dim(
            block_order[:count], member * per_owner, per_owner, 1
        )
        every = np.arange(n_members * span_dev, dtype=np.int32)
        pick = (owned_rows(order)[..., None] == every).reshape(
            count * span_dev, n_members, 1, span_dev
        )
        tick = np.arange(count, dtype=np.int32)
        same = np.repeat(tick, span_dev)[:, None, None, None] == tick[None, None, :, None]
        return (pick & same).astype(jnp.bfloat16).reshape(count * span_dev, -1)

    def deliver_early(gathered, pick):
        picked = matmul(pick, gathered.reshape(-1, kv_width)).astype(jnp.bfloat16)
        return picked.reshape(-1, span_dev, kv_width)

    def late_picks(block_order):
        order = block_order[-1].reshape(n_planes, n_columns, per_owner)
        order = lax.dynamic_index_in_dim(order, column, 1, keepdims=False)
        held = plane * n_columns * span_dev + np.arange(n_columns * span_dev, dtype=np.int32)
        pick = (owned_rows(order)[..., None] == held).astype(jnp.bfloat16)
        return pick.reshape(n_planes * span_dev, n_columns * span_dev)

    half = model_width // 2
    slots = experts * capacity
    tick_rows = []
    gains = (attn_gain, kv_gain)
    flops = 2 * 3 * n_columns * slots * model_width * local_gate.shape[1]
    for tick in range(n_sections):
        last_tick = tick + 1 == n_sections
        tokens = jnp.where(is_first, spans[tick], layer_in) if tick else spans[0]
        tick_rows.append(tokens)
        if last_tick:
            late_rows = project(EARLY, n_sections, gains, latent_full, turns)
            late_rows = jnp.pad(late_rows, ((0, 0), (0, half - kv_width)))
            tokens, late_rows = lax.optimization_barrier((tokens, late_rows))
        chosen = in_vmem(
            choose_kernel if tick else first_choose_kernel,
            jax.ShapeDtypeStruct((2 * slots, half), jnp.bfloat16),
            (tokens, moe_gain) if tick else (moe_gain,),
            8,
            tick=tick,
            tables=(hits,) if tick else (spans, own_ids),
        )
        if tick == 0:
            held = (chosen, offsets, own_ids, gate_vals, owner_map, section_id == 0)
            held = lax.optimization_barrier(held)
            chosen, offsets, own_ids, gate_vals, owner_map, is_first = held
            routes = jnp.concatenate([own_ids, by_tick(gate_vals[0])], axis=2)
            block_order = by_tick(owner_map[0])
            picks = early_picks(block_order, EARLY), late_picks(block_order)
            table = jax.ShapeDtypeStruct((n_sections, span_dev, 4 * slots), jnp.float32)
            make = functools.partial(table_kernel, 2 * slots)
            hits, weighs = in_vmem(make, [table] * 2, (routes,), 8)
            positions = by_tick(offsets)[:, None] + member * span_dev
            positions = positions + jnp.arange(span_dev, dtype=jnp.int32)[None, :]
            turns = rotation(kv_width - LAT, positions.reshape(-1))
        arrived = lax.all_to_all(chosen, "z", split_axis=0, concat_axis=0, tiled=True)
        if last_tick:
            arrived = jnp.concatenate([arrived, late_rows], axis=0)
        if tick == 0:
            held = (arrived, turns, hits, weighs, picks, tokens)
            held = lax.optimization_barrier(held)
            arrived, turns, hits, weighs, picks, tokens = held
        token_rows = lax.all_gather(arrived, "y", axis=0, tiled=True)
        parts = in_vmem(
            lambda *refs: expert_kernel(n_columns, *refs),
            jax.ShapeDtypeStruct((n_columns * slots, model_width), jnp.bfloat16),
            (token_rows, local_gate, local_up, local_down),
            24,
            flops,
        )
        if tick == 1:
            parts, latent_full = lax.optimization_barrier((parts, latent_full))
        if tick == EARLY - 1:
            held = lax.optimization_barrier((parts, tick_rows, gains, latent_full, turns))
            parts, tick_rows, gains, latent_full, turns = held
            early_rows = project(0, EARLY, gains, latent_full, turns)
            parts, early_rows = lax.optimization_barrier((parts, early_rows))
            early = lax.all_gather(early_rows, ("z", "y"), axis=0)
        quarters = lax.all_to_all(parts, "y", split_axis=0, concat_axis=0, tiled=True)
        if last_tick:
            quarters, early = lax.optimization_barrier((quarters, early))
        summed = in_vmem(
            functools.partial(total_kernel, n_columns),
            jax.ShapeDtypeStruct(((4 if last_tick else 2) * slots, half), jnp.bfloat16),
            (quarters, token_rows, picks[1]) if last_tick else (quarters,),
            12,
        )
        returned = lax.all_to_all(summed, "z", split_axis=0, concat_axis=0, tiled=True)
        if last_tick:
            returned = returned.reshape(n_planes, -1, half)
            late = jnp.sum(returned[:, -8:, :kv_width].astype(jnp.float32), axis=0)
            late = late.astype(jnp.bfloat16)[None]
            returned = returned[:, :-8].reshape(-1, half)
        layer_out = in_vmem(
            combine_kernel,
            jax.ShapeDtypeStruct((span_dev, model_width), jnp.bfloat16),
            (tokens, returned),
            8,
            tick=tick,
            tables=(weighs,),
        )
        if not last_tick:
            layer_in = shifted(layer_out, "section", 1)
    early = deliver_early(early, picks[0])
    delivered = [early, late]
    blank = jnp.zeros((n_spans, span_dev, kv_width), jnp.bfloat16)
    kv_ticks = jnp.concatenate(delivered + [blank], axis=0)
    kv_store = lax.dynamic_slice_in_dim(kv_ticks, section_id, n_spans, 0)
    return (layer_out[None], kv_store[None])


def solution(mesh):
    n_members = mesh.shape["ep"]
    grid = Mesh(
        mesh.devices.reshape(mesh.shape["section"], n_members // EXP_SPLIT, EXP_SPLIT),
        ("section", "z", "y"),
    )
    ep = ("z", "y")
    in_specs = (
        P(None, ep, None),
        P("section", None),
        P("section", None),
        P("section", None),
        P("section", ep, None),
        P("section", None, ep),
        P("section", None, ep),
        P("section", ep, None),
        P("section", None, None, None),
        P("section", None, ep, None),
        P("section", None, None),
        P(),
    )
    out_specs = (P("section", ep, None), P("section", None, ep, None))
    return jax.shard_map(body, mesh=grid, in_specs=in_specs, out_specs=out_specs, check_vma=False)
```
